32 devices in a mesh: member: 2 (over x), tile: 16 (over z, y, core).
Axes of the slice: x: 2, y: 2, z: 4, core: 2. Of those that a mesh axis runs over, the one named last changes fastest.
Arguments:
- noise_seeds: int32 [4], P('member'), parts along dimension 0, may hold values from 0 to 2147483646
- diffusivity: float32 [128, 256], P('tile'), may hold values from 0.03 to 0.24
- wet_mask: int32 [128, 256], P('tile'), may hold values 0 or 1
- vert_factor: float32 [75, 75], replicated, may hold values from -0.75 to 0.75
- norm_scale: float32 [128, 256], P('tile'), may hold values from 0.5 to 8
- obs_cell: int32 [16, 16, 128], P('tile'), may hold values from 0 to 2046, as said below
- obs_frac: float32 [16, 16, 2, 128], P('tile'), may hold values from 0 to 1
- obs_count: int32 [16, 16], P('tile'), may hold values from 32 to 128, as said below
Outputs:
- perturbation: bfloat16 [150, 128, 256], P('member', 'tile'), parts along dimension 0
- profiles: bfloat16 [16, 16, 150, 128], P('tile', None, 'member'), parts along dimension 2
The draws below stay inside these ranges and needn't reach their ends.
There are 2 independent parts, one for each index of `member`. The reference program is written for one: setup_inputs(seed, part) draws one part's arguments, and reference() takes and returns one part's arrays. A program takes and returns all parts, laid end to end along the dimension named above; an argument that names none is the same for every part. Nothing has to cross between parts.
Inputs may be any that keep to these rules, and one draw needn't show every extreme that they name: `obs_cell`: each entry is row * 256 + column of an anchor cell in the owner tile's block of 8 x 256 cells, with column below 255, and row below 7 where the owner is the last tile. `obs_count`: some owner receives 128 live slots from every holder, and other counts vary by owner.
All inputs are finite; a program needn't handle non-finite values. No bound on the sum of `wet_mask` on one device may be relied on, other than what follows from the above.
Results may differ from the reference program's by a relative error of at most 0.0045.
Values may be sent and summed in bfloat16 or wider, within the bound.
A program may use at most 64 MiB of HBM per device.

```python
import math
import jax
import jax.numpy as jnp
from jax import lax

L = 75
STEPS = 8
RY = 8
NX = 256
CAP = 128
NY = 128
N_TILE = 16


def draw_obs_cell(key, part):
    owner = jnp.arange(N_TILE, dtype=jnp.int32)[None, :, None]
    row_top = jnp.where(owner == N_TILE - 1, RY - 1, RY).astype(jnp.int32)
    row_top = jnp.broadcast_to(row_top, (N_TILE, N_TILE, CAP))
    rows_drawn = jax.random.randint(jax.random.fold_in(key, 11), (N_TILE, N_TILE, CAP), 0, row_top, dtype=jnp.int32)
    cols_drawn = jax.random.randint(jax.random.fold_in(key, 12), (N_TILE, N_TILE, CAP), 0, NX - 1, dtype=jnp.int32)
    return rows_drawn * NX + cols_drawn


def draw_obs_count(key, part):
    base_counts = jax.random.randint(jax.random.fold_in(key, 21), (N_TILE, N_TILE), CAP // 4, CAP // 2 + 1, dtype=jnp.int32)
    busy_counts = jax.random.randint(jax.random.fold_in(key, 22), (N_TILE, N_TILE), CAP // 2, CAP + 1, dtype=jnp.int32)
    hot_owners = jax.random.randint(jax.random.fold_in(key, 23), (3,), 0, N_TILE, dtype=jnp.int32)
    owner_ids = jnp.arange(N_TILE, dtype=jnp.int32)
    is_hot = jnp.any(owner_ids[None, :] == hot_owners[:, None], axis=0)
    counts = jnp.where(is_hot[None, :], busy_counts, base_counts)
    counts = jnp.where(owner_ids[None, :] == hot_owners[0], CAP, counts)
    corner = jax.random.randint(jax.random.fold_in(key, 24), (2,), 0, N_TILE, dtype=jnp.int32)
    counts = counts.at[corner[0], corner[1]].set(CAP)
    return counts.astype(jnp.int32)


def with_ends(values, stream_key, least, high):
    longest = values.shape.index(max(values.shape))
    spots = []
    for shift in (0, 1):
        where = [jax.random.randint(jax.random.fold_in(stream_key, axis), (), 0, length) for axis, length in enumerate(values.shape)]
        where[longest] = (where[longest] + shift) % values.shape[longest]
        spots.append(tuple(where))
    return values.at[spots[0]].set(least).at[spots[1]].set(high)


def block_scale(stream_key, extent, shards, smallest, high):
    level, own = 1.0, jax.random.fold_in(stream_key, 6)
    for dim, blocks in shards:
        heights = jnp.exp(jax.random.uniform(jax.random.fold_in(own, dim), (blocks,), jnp.float32, smallest / len(shards), high / len(shards)))
        level = level * jnp.repeat(heights, extent[dim] // blocks).reshape([-1 if axis == dim else 1 for axis in range(len(extent))])
    return level


def scatter_about(stream_key, shape, scale, bound, kind=jnp.bfloat16):
    return jnp.clip(scale * jax.random.normal(stream_key, shape, jnp.float32), -bound, bound).astype(kind)


def setup_inputs(seed: int = 0, part: int = 0) -> dict:
    key_of = jax.random.split(jax.random.key(seed), 9)
    part_splits = jax.random.split(jax.random.fold_in(key_of[8], part), 9)
    noise_seeds = jax.random.randint(part_splits[0], (2,), 0, 2147483647).astype(jnp.int32)
    diffusivity = jnp.clip(jnp.exp(math.log(0.24) - 2.0794415 * jax.random.uniform(key_of[1], (NY, NX), jnp.float32) ** block_scale(key_of[1], (NY, NX), ((0, 16),), -0.2, 0.2)), 0.03, 0.24)
    wet_mask = with_ends((jax.random.randint(key_of[2], (NY, NX), 0, 10) < 7).astype(jnp.int32), jax.random.fold_in(key_of[2], 1), 0, 1)
    vert_factor = scatter_about(key_of[3], (L, L), L ** -0.5, 0.75, jnp.float32)
    norm_scale = jnp.clip(jnp.exp(math.log(8.0) - 2.7725887 * jax.random.uniform(key_of[4], (NY, NX), jnp.float32) ** block_scale(key_of[4], (NY, NX), ((0, 16),), -0.2, 0.2)), 0.5, 8.0)
    obs_cell = draw_obs_cell(jax.random.fold_in(key_of[8], 71), part)
    obs_frac = jnp.clip(1.0 * jax.random.uniform(key_of[6], (N_TILE, N_TILE, 2, CAP), jnp.float32) ** block_scale(key_of[6], (N_TILE, N_TILE, 2, CAP), ((0, 16),), -0.2, 0.2), 0.0, 1.0)
    obs_count = draw_obs_count(jax.random.fold_in(key_of[8], 71), part)
    return {"noise_seeds": noise_seeds, "diffusivity": diffusivity, "wet_mask": wet_mask, "vert_factor": vert_factor, "norm_scale": norm_scale, "obs_cell": obs_cell, "obs_frac": obs_frac, "obs_count": obs_count}


def scramble(hashed):
    hashed = jnp.bitwise_xor(hashed, hashed >> 16 & 65535) * -2048144789
    hashed = jnp.bitwise_xor(hashed, hashed >> 13 & 524287) * -1028477387
    return jnp.bitwise_xor(hashed, hashed >> 16 & 65535)

def cell_noise(noise_seeds, counter):
    hashed = scramble(counter * -1640531535 + noise_seeds[0])
    hashed = scramble(jnp.bitwise_xor(hashed, noise_seeds[1]))
    uniform = ((hashed >> 8 & 16777215).astype(jnp.float32) + 0.5) * (1.0 / 16777216.0)
    return (uniform - 0.5) * 3.4641016151377544

def face_terms(wet_pad):
    face_rows = jnp.sqrt(wet_pad[1:] * wet_pad[:-1])
    face_cols = jnp.sqrt(wet_pad[:, 1:] * wet_pad[:, :-1])
    return (face_rows, face_cols)

def diffuse(padded, face_rows, face_cols):
    flux_rows = face_rows[None] * (padded[:, 1:] - padded[:, :-1])
    flux_cols = face_cols[None] * (padded[:, :, 1:] - padded[:, :, :-1])
    zero_col = jnp.zeros(flux_cols.shape[:2] + (1,), jnp.float32)
    net_cols = jnp.concatenate([flux_cols, zero_col], 2) - jnp.concatenate([zero_col, flux_cols], 2)
    return padded[:, 1:-1] + (flux_rows[:, 1:] - flux_rows[:, :-1]) + net_cols[:, 1:-1]

def bilinear(flat_field, anchor, frac_y, frac_x, columns):
    corner_nw = jnp.take(flat_field, anchor, axis=1).astype(jnp.float32)
    corner_ne = jnp.take(flat_field, anchor + 1, axis=1).astype(jnp.float32)
    corner_sw = jnp.take(flat_field, anchor + columns, axis=1).astype(jnp.float32)
    corner_se = jnp.take(flat_field, anchor + columns + 1, axis=1).astype(jnp.float32)
    blended = (1.0 - frac_y) * ((1.0 - frac_x) * corner_nw + frac_x * corner_ne) + frac_y * ((1.0 - frac_x) * corner_sw + frac_x * corner_se)
    return blended

def reference(noise_seeds, diffusivity, wet_mask, vert_factor, norm_scale, obs_cell, obs_frac, obs_count):
    wet_float = wet_mask.astype(jnp.float32)
    wet_kappa = diffusivity * wet_float
    wet_pad = jnp.pad(wet_kappa, ((1, 1), (0, 0)))
    face_rows, face_cols = face_terms(wet_pad)
    level_ids = lax.broadcasted_iota(jnp.int32, (L, NY, NX), 0)
    row_ids = lax.broadcasted_iota(jnp.int32, (L, NY, NX), 1)
    col_ids = lax.broadcasted_iota(jnp.int32, (L, NY, NX), 2)
    counter = (level_ids * NY + row_ids) * NX + col_ids
    state_field = cell_noise(noise_seeds, counter) * wet_float[None]
    for outer_step in range(STEPS):
        padded = jnp.pad(state_field, ((0, 0), (1, 1), (0, 0)))
        state_field = diffuse(padded, face_rows, face_cols)
    mixed_levels = jnp.dot(vert_factor, state_field.reshape(L, NY * NX), precision=lax.Precision.HIGHEST, preferred_element_type=jnp.float32)
    perturbation = (mixed_levels.reshape(L, NY, NX) * norm_scale[None]).astype(jnp.bfloat16)
    flat_field = jnp.concatenate([perturbation, jnp.zeros((L, 1, NX), jnp.bfloat16)], 1).reshape(L, (NY + 1) * NX)
    owner_base = (jnp.arange(N_TILE, dtype=jnp.int32) * (RY * NX)).astype(jnp.int32)
    slot_ids = jnp.arange(CAP, dtype=jnp.int32)

    def one_holder(inputs):
        cells, fracs, counts = inputs
        anchor = (cells + owner_base[:, None]).astype(jnp.int32)
        blended = bilinear(flat_field, anchor, fracs[:, 0], fracs[:, 1], NX)
        profile = jnp.transpose(blended, (1, 0, 2)).astype(jnp.bfloat16)
        live_slot = slot_ids[None, None, :] < counts[:, None, None]
        return jnp.where(live_slot, profile, jnp.zeros_like(profile))
    profiles = lax.map(one_holder, (obs_cell, obs_frac, obs_count))
    return (perturbation, profiles)
```

```python
import functools

import jax
import jax.numpy as jnp
from jax import lax
from jax.experimental import pallas as pl
from jax.experimental.pallas import tpu as pltpu
from jax.sharding import PartitionSpec as P

STEPS = 8
GROUP = 8
SPREAD = 3.4641016151377544
MESH = pl.DeviceIdType.MESH


def scramble(hashed):
    hashed = (hashed ^ lax.shift_right_logical(hashed, jnp.int32(16))) * jnp.int32(-2048144789)
    hashed = (hashed ^ lax.shift_right_logical(hashed, jnp.int32(13))) * jnp.int32(-1028477387)
    return hashed ^ lax.shift_right_logical(hashed, jnp.int32(16))


def kernel(
    n,
    seeds_ref,
    count_ref,
    diff_ref,
    wet_ref,
    vert_ref,
    scale_ref,
    cell_ref,
    frac_ref,
    pert_ref,
    prof_ref,
    edge_send,
    above_recv,
    below_recv,
    next_recv,
    probe_send,
    probe_recv,
    noise,
    face_rows,
    face_cols,
    wet_all,
    state,
    vert_pad,
    field,
    field_rows,
    prof_send,
    prof_recv,
    edge_ss,
    edge_rs,
    probe_ss,
    probe_rs,
    prof_ss,
    prof_rs,
):
    me = lax.axis_index("tile")
    rows, cols = diff_ref.shape
    levels = vert_ref.shape[0]
    padded = state.shape[1]
    groups = padded // GROUP
    slots = cell_ref.shape[2]
    total_rows = n * rows
    span = rows + 2 * STEPS + 1
    kept = rows + 1

    barrier = pltpu.get_barrier_semaphore()

    def greet(k, carry):
        peer = lax.rem(me + k, n)
        pl.semaphore_signal(barrier, inc=1, device_id={"tile": peer}, device_id_type=MESH)
        return carry

    lax.fori_loop(1, n, greet, 0)

    kappa = diff_ref[...] * wet_ref[...].astype(jnp.float32)
    edge_send[0:rows, :] = kappa
    edge_send[rows : 2 * rows, :] = scale_ref[...]
    slot_ids = lax.broadcasted_iota(jnp.int32, (1, slots), 1)

    def pack(h, carry):
        anchor = cell_ref[0, pl.ds(h, 1), :]
        frac = frac_ref[0, h]
        row = lax.shift_right_logical(anchor, jnp.int32(cols.bit_length() - 1))
        col = anchor - row * cols
        live = jnp.where(slot_ids < count_ref[0, h], 1.0, 0.0)
        frac_y = frac[0:1, :]
        probe_send[h, 0:1, :] = col.astype(jnp.float32)
        probe_send[h, 1:2, :] = frac[1:2, :]
        probe_send[h, 2:3, :] = row.astype(jnp.float32)
        probe_send[h, 3:4, :] = (1.0 - frac_y) * live
        probe_send[h, 4:5, :] = frac_y * live
        probe_send[h, 5:8, :] = jnp.zeros((3, slots), jnp.float32)
        return carry

    lax.fori_loop(0, n, pack, 0)

    seed_a = seeds_ref[0]
    seed_b = seeds_ref[1]
    shape = (GROUP, cols)
    spread_ids = (
        lax.broadcasted_iota(jnp.int32, shape, 0) * (total_rows * cols)
        + lax.broadcasted_iota(jnp.int32, shape, 1)
    ) * jnp.int32(-1640531535)
    first_row = me * rows - STEPS

    def draw(g, carry):
        at = pl.multiple_of(g * GROUP, GROUP)
        for j in range(span):
            base = (g * (GROUP * total_rows) + first_row + j) * cols
            hashed = scramble(spread_ids + (base * jnp.int32(-1640531535) + seed_a))
            hashed = scramble(hashed ^ seed_b)
            drawn = lax.shift_right_logical(hashed, jnp.int32(8)).astype(jnp.float32)
            noise[j, pl.ds(at, GROUP), :] = drawn * (SPREAD / 16777216.0) + SPREAD * (
                0.5 / 16777216.0 - 0.5
            )
        return carry

    lax.fori_loop(0, groups // 2, draw, 0)

    pl.semaphore_wait(barrier, n - 1)

    def edge_copy(which):
        if which == 0:
            src, dst, by = edge_send.at[pl.ds(0, rows)], above_recv, 1
        elif which == 1:
            src, dst, by = edge_send, below_recv, n - 1
        else:
            src, dst, by = edge_send.at[pl.ds(0, rows)], next_recv, n - 2
        return pltpu.make_async_remote_copy(
            src_ref=src,
            dst_ref=dst,
            send_sem=edge_ss.at[which],
            recv_sem=edge_rs.at[which],
            device_id={"tile": lax.rem(me + by, n)},
            device_id_type=MESH,
        )

    def probe_copy(peer, slot):
        return pltpu.make_async_remote_copy(
            src_ref=probe_send.at[peer],
            dst_ref=probe_recv.at[slot],
            send_sem=probe_ss.at[peer],
            recv_sem=probe_rs.at[slot],
            device_id={"tile": peer},
            device_id_type=MESH,
        )

    for which in range(3):
        edge_copy(which).start()

    def send_probe(k, carry):
        probe_copy(lax.rem(me + k, n), me).start()
        return carry

    lax.fori_loop(1, n, send_probe, 0)
    probe_recv[me] = probe_send[me]

    lax.fori_loop(groups // 2, groups, draw, 0)

    vert_pad[...] = jnp.zeros_like(vert_pad)
    vert_pad[0:levels, 0:levels] = vert_ref[...]
    vert = vert_pad[:, 0:padded]
    vert_hi = vert.astype(jnp.bfloat16)
    vert_lo = (vert - vert_hi.astype(jnp.float32)).astype(jnp.bfloat16)

    for which in range(3):
        edge_copy(which).wait_recv()

    zero = jnp.zeros((rows, cols), jnp.float32)
    kappa_all = jnp.concatenate(
        [
            jnp.where(me > 0, above_recv[...], zero),
            edge_send[0:rows, :],
            jnp.where(me < n - 1, below_recv[0:rows, :], zero),
            jnp.where(me < n - 2, next_recv[...], zero),
        ],
        0,
    )
    wet = jnp.where(kappa_all > 0.0, 1.0, 0.0)
    kappa_next = pltpu.roll(kappa_all, cols - 1, 1)
    last = lax.broadcasted_iota(jnp.int32, kappa_all.shape, 1) == cols - 1
    faces_c = jnp.where(last, 0.0, jnp.sqrt(kappa_all * kappa_next))
    faces_r = jnp.sqrt(kappa_all[0 : span - 1] * kappa_all[1:span])
    for j in range(span):
        wet_all[j] = jnp.broadcast_to(wet[j : j + 1], shape)
        face_cols[j] = jnp.broadcast_to(faces_c[j : j + 1], shape)
        if j < span - 1:
            face_rows[j] = jnp.broadcast_to(faces_r[j : j + 1], shape)

    def diffuse(g, carry):
        at = pl.multiple_of(g * GROUP, GROUP)
        old = [noise[j, pl.ds(at, GROUP), :] * wet_all[j] for j in range(span)]
        for step in range(STEPS):
            new = list(old)
            flux_up = face_rows[step] * (old[step + 1] - old[step])
            for j in range(step + 1, span - 1 - step):
                here = old[j]
                flux_down = face_rows[j] * (old[j + 1] - here)
                flux = face_cols[j] * (pltpu.roll(here, cols - 1, 1) - here)
                new[j] = here + (flux_down - flux_up) + (flux - pltpu.roll(flux, 1, 1))
                flux_up = flux_down
            old = new
        for r in range(kept):
            state[r, pl.ds(at, GROUP), :] = old[STEPS + r]
        return carry

    lax.fori_loop(0, groups, diffuse, 0)

    for r in range(kept):
        value = state[r]
        high = value.astype(jnp.bfloat16)
        low = (value - high.astype(jnp.float32)).astype(jnp.bfloat16)
        dot = functools.partial(jnp.dot, preferred_element_type=jnp.float32)
        mixed = dot(vert_hi, high) + (dot(vert_hi, low) + dot(vert_lo, high))
        if r < rows:
            scale = scale_ref[r : r + 1, :]
        else:
            scale = below_recv[rows : rows + 1, :]
        field[r * padded : (r + 1) * padded, :] = (mixed * scale).astype(jnp.bfloat16)

    def await_probe(k, carry):
        source = lax.rem(me + k, n)
        probe_copy(source, source).wait_recv()
        return carry

    lax.fori_loop(1, n, await_probe, 0)

    col_ids = lax.broadcasted_iota(jnp.int32, (cols, 2 * slots), 0).astype(jnp.float32)

    def answer(pair):
        probes = jnp.concatenate([probe_recv[2 * pair], probe_recv[2 * pair + 1]], 1)
        col, frac_x, row = probes[0:1], probes[1:2], probes[2:3]
        top, bottom = probes[3:4], probes[4:5]
        weights = jnp.where(
            col_ids == col, 1.0 - frac_x, jnp.where(col_ids == col + 1.0, frac_x, 0.0)
        ).astype(jnp.bfloat16)
        across = jnp.dot(field[...], weights, preferred_element_type=jnp.float32)
        total = None
        for r in range(kept):
            share = jnp.where(row == float(r), top, jnp.where(row == float(r - 1), bottom, 0.0))
            term = across[r * padded : (r + 1) * padded] * share
            total = term if total is None else total + term
        total = total.astype(jnp.bfloat16)
        prof_send[2 * pair] = total[:, 0:slots]
        prof_send[2 * pair + 1] = total[:, slots : 2 * slots]

    def prof_copy(peer, slot):
        return pltpu.make_async_remote_copy(
            src_ref=prof_send.at[peer],
            dst_ref=prof_recv.at[slot],
            send_sem=prof_ss.at[peer],
            recv_sem=prof_rs.at[slot],
            device_id={"tile": peer},
            device_id_type=MESH,
        )

    pairs = n // 2
    my_pair = me // 2

    def answer_other(k, carry):
        pair = lax.rem(my_pair + k, pairs)
        answer(pair)
        prof_copy(2 * pair, me).start()
        prof_copy(2 * pair + 1, me).start()
        return carry

    lax.fori_loop(1, pairs, answer_other, 0)
    answer(my_pair)
    prof_copy(4 * my_pair + 1 - me, me).start()
    prof_ref[0, me] = prof_send[me, 0:levels, :]

    for r in range(rows):
        field_rows[:, r, :] = field[r * padded : (r + 1) * padded, :].astype(jnp.float32)
    pert_ref[...] = field_rows[0:levels].astype(jnp.bfloat16)

    def finish(k, carry):
        source = lax.rem(me + n - k, n)
        prof_copy(source, source).wait_recv()
        prof_ref[0, source] = prof_recv[source, 0:levels, :]
        return carry

    lax.fori_loop(1, n, finish, 0)

    def settle(k, carry):
        peer = lax.rem(me + k, n)
        probe_copy(peer, me).wait_send()
        prof_copy(peer, me).wait_send()
        return carry

    lax.fori_loop(1, n, settle, 0)
    for which in range(3):
        edge_copy(which).wait_send()


def body(
    noise_seeds, diffusivity, wet_mask, vert_factor, norm_scale, obs_cell, obs_frac, obs_count
):
    rows, cols = diffusivity.shape
    levels = vert_factor.shape[0]
    n = lax.axis_size("tile")
    slots = obs_cell.shape[2]
    if rows != STEPS or n % 2 or cols & (cols - 1):
        raise ValueError("unsupported sizes")
    padded = -(-levels // 16) * 16
    span = rows + 2 * STEPS + 1
    kept = rows + 1
    f32, bf16 = jnp.float32, jnp.bfloat16
    vmem = pl.BlockSpec(memory_space=pltpu.VMEM)
    smem = pl.BlockSpec(memory_space=pltpu.SMEM)
    dma = pltpu.SemaphoreType.DMA
    return pl.pallas_call(
        functools.partial(kernel, n),
        out_shape=(
            jax.ShapeDtypeStruct((levels, rows, cols), bf16),
            jax.ShapeDtypeStruct((1, n, levels, slots), bf16),
        ),
        in_specs=[smem, smem] + [vmem] * 6,
        out_specs=(vmem, vmem),
        scratch_shapes=[
            pltpu.VMEM((2 * rows, cols), f32),
            pltpu.VMEM((rows, cols), f32),
            pltpu.VMEM((2 * rows, cols), f32),
            pltpu.VMEM((rows, cols), f32),
            pltpu.VMEM((n, 8, slots), f32),
            pltpu.VMEM((n, 8, slots), f32),
            pltpu.VMEM((span, padded, cols), f32),
            pltpu.VMEM((span, GROUP, cols), f32),
            pltpu.VMEM((span, GROUP, cols), f32),
            pltpu.VMEM((span, GROUP, cols), f32),
            pltpu.VMEM((kept, padded, cols), f32),
            pltpu.VMEM((padded, 128), f32),
            pltpu.VMEM((kept * padded, cols), bf16),
            pltpu.VMEM((padded, rows, cols), f32),
            pltpu.VMEM((n, padded, slots), bf16),
            pltpu.VMEM((n, padded, slots), bf16),
            dma((3,)),
            dma((3,)),
            dma((n,)),
            dma((n,)),
            dma((n,)),
            dma((n,)),
        ],
        compiler_params=pltpu.CompilerParams(
            collective_id=0, has_side_effects=True, vmem_limit_bytes=32 * 1024 * 1024
        ),
    )(
        noise_seeds,
        obs_count,
        diffusivity,
        wet_mask,
        vert_factor,
        norm_scale,
        obs_cell,
        obs_frac,
    )


def solution(mesh):
    in_specs = (
        P("member"),
        P("tile", None),
        P("tile", None),
        P(),
        P("tile", None),
        P("tile", None, None),
        P("tile", None, None, None),
        P("tile", None),
    )
    out_specs = (P("member", "tile", None), P("tile", None, "member", None))
    return jax.shard_map(body, mesh=mesh, in_specs=in_specs, out_specs=out_specs, check_vma=False)
```

```python
import functools

import jax
import jax.numpy as jnp
from jax import lax
from jax.experimental import pallas as pl
from jax.experimental.pallas import tpu as pltpu
from jax.sharding import PartitionSpec as P

STEPS = 8
GROUP = 8
SPREAD = 3.4641016151377544
MESH = pl.DeviceIdType.MESH


def scramble(hashed):
    hashed = (hashed ^ lax.shift_right_logical(hashed, jnp.int32(16))) * jnp.int32(-2048144789)
    hashed = (hashed ^ lax.shift_right_logical(hashed, jnp.int32(13))) * jnp.int32(-1028477387)
    return hashed ^ lax.shift_right_logical(hashed, jnp.int32(16))


def kernel(
    n,
    seeds_hbm,
    count_hbm,
    diff_hbm,
    wet_hbm,
    vert_hbm,
    scale_hbm,
    cell_hbm,
    frac_hbm,
    pert_ref,
    prof_ref,
    seeds_ref,
    count_ref,
    diff_ref,
    wet_ref,
    vert_ref,
    scale_ref,
    cell_ref,
    frac_ref,
    in_sems,
    edge_send,
    above_recv,
    below_recv,
    next_recv,
    probe_send,
    probe_recv,
    noise,
    face_rows,
    face_cols,
    wet_all,
    state,
    vert_pad,
    field,
    field_rows,
    prof_send,
    prof_recv,
    edge_ss,
    edge_rs,
    probe_ss,
    probe_rs,
    prof_ss,
    prof_rs,
):
    pulls = [
        pltpu.make_async_copy(src, dst, in_sems.at[k])
        for k, (src, dst) in enumerate(
            (
                (diff_hbm, diff_ref),
                (wet_hbm, wet_ref),
                (scale_hbm, scale_ref),
                (seeds_hbm, seeds_ref),
                (count_hbm, count_ref),
                (cell_hbm, cell_ref),
                (frac_hbm, frac_ref),
                (vert_hbm, vert_ref),
            )
        )
    ]
    for pull in pulls:
        pull.start()

    me = lax.axis_index("tile")
    rows, cols = diff_ref.shape
    levels = vert_ref.shape[0]
    padded = state.shape[1]
    groups = padded // GROUP
    slots = cell_ref.shape[2]
    total_rows = n * rows
    span = rows + 2 * STEPS + 1
    kept = rows + 1

    barrier = pltpu.get_barrier_semaphore()

    def greet(k, carry):
        peer = lax.rem(me + k, n)
        pl.semaphore_signal(barrier, inc=1, device_id={"tile": peer}, device_id_type=MESH)
        return carry

    lax.fori_loop(1, n, greet, 0)

    for pull in pulls:
        pull.wait()

    kappa = diff_ref[...] * wet_ref[...].astype(jnp.float32)
    edge_send[0:rows, :] = kappa
    edge_send[rows : 2 * rows, :] = scale_ref[...]
    slot_ids = lax.broadcasted_iota(jnp.int32, (1, slots), 1)

    def pack(h, carry):
        anchor = cell_ref[0, pl.ds(h, 1), :]
        frac = frac_ref[0, h]
        row = lax.shift_right_logical(anchor, jnp.int32(cols.bit_length() - 1))
        col = anchor - row * cols
        live = jnp.where(slot_ids < count_ref[0, h], 1.0, 0.0)
        frac_y = frac[0:1, :]
        probe_send[h, 0:1, :] = col.astype(jnp.float32)
        probe_send[h, 1:2, :] = frac[1:2, :]
        probe_send[h, 2:3, :] = row.astype(jnp.float32)
        probe_send[h, 3:4, :] = (1.0 - frac_y) * live
        probe_send[h, 4:5, :] = frac_y * live
        probe_send[h, 5:8, :] = jnp.zeros((3, slots), jnp.float32)
        return carry

    lax.fori_loop(0, n, pack, 0)

    seed_a = seeds_ref[0]
    seed_b = seeds_ref[1]
    shape = (GROUP, cols)
    spread_ids = (
        lax.broadcasted_iota(jnp.int32, shape, 0) * (total_rows * cols)
        + lax.broadcasted_iota(jnp.int32, shape, 1)
    ) * jnp.int32(-1640531535)
    first_row = me * rows - STEPS

    def draw(g, carry):
        at = pl.multiple_of(g * GROUP, GROUP)
        for j in range(span):
            base = (g * (GROUP * total_rows) + first_row + j) * cols
            hashed = scramble(spread_ids + (base * jnp.int32(-1640531535) + seed_a))
            hashed = scramble(hashed ^ seed_b)
            drawn = lax.shift_right_logical(hashed, jnp.int32(8)).astype(jnp.float32)
            noise[j, pl.ds(at, GROUP), :] = drawn * (SPREAD / 16777216.0) + SPREAD * (
                0.5 / 16777216.0 - 0.5
            )
        return carry

    lax.fori_loop(0, groups // 2, draw, 0)

    pl.semaphore_wait(barrier, n - 1)

    def edge_copy(which):
        if which == 0:
            src, dst, by = edge_send.at[pl.ds(0, rows)], above_recv, 1
        elif which == 1:
            src, dst, by = edge_send, below_recv, n - 1
        else:
            src, dst, by = edge_send.at[pl.ds(0, rows)], next_recv, n - 2
        return pltpu.make_async_remote_copy(
            src_ref=src,
            dst_ref=dst,
            send_sem=edge_ss.at[which],
            recv_sem=edge_rs.at[which],
            device_id={"tile": lax.rem(me + by, n)},
            device_id_type=MESH,
        )

    def probe_copy(peer, slot):
        return pltpu.make_async_remote_copy(
            src_ref=probe_send.at[peer],
            dst_ref=probe_recv.at[slot],
            send_sem=probe_ss.at[peer],
            recv_sem=probe_rs.at[slot],
            device_id={"tile": peer},
            device_id_type=MESH,
        )

    for which in range(3):
        edge_copy(which).start()

    def send_probe(k, carry):
        probe_copy(lax.rem(me + k, n), me).start()
        return carry

    lax.fori_loop(1, n, send_probe, 0)
    probe_recv[me] = probe_send[me]

    lax.fori_loop(groups // 2, groups, draw, 0)

    vert_pad[...] = jnp.zeros_like(vert_pad)
    vert_pad[0:levels, 0:levels] = vert_ref[...]
    vert = vert_pad[:, 0:padded]
    vert_hi = vert.astype(jnp.bfloat16)
    vert_lo = (vert - vert_hi.astype(jnp.float32)).astype(jnp.bfloat16)

    for which in range(3):
        edge_copy(which).wait_recv()

    zero = jnp.zeros((rows, cols), jnp.float32)
    kappa_all = jnp.concatenate(
        [
            jnp.where(me > 0, above_recv[...], zero),
            edge_send[0:rows, :],
            jnp.where(me < n - 1, below_recv[0:rows, :], zero),
            jnp.where(me < n - 2, next_recv[...], zero),
        ],
        0,
    )
    wet = jnp.where(kappa_all > 0.0, 1.0, 0.0)
    kappa_next = pltpu.roll(kappa_all, cols - 1, 1)
    last = lax.broadcasted_iota(jnp.int32, kappa_all.shape, 1) == cols - 1
    faces_c = jnp.where(last, 0.0, jnp.sqrt(kappa_all * kappa_next))
    faces_r = jnp.sqrt(kappa_all[0 : span - 1] * kappa_all[1:span])
    for j in range(span):
        wet_all[j] = jnp.broadcast_to(wet[j : j + 1], shape)
        face_cols[j] = jnp.broadcast_to(faces_c[j : j + 1], shape)
        if j < span - 1:
            face_rows[j] = jnp.broadcast_to(faces_r[j : j + 1], shape)

    def diffuse(g, carry):
        at = pl.multiple_of(g * GROUP, GROUP)
        old = [noise[j, pl.ds(at, GROUP), :] * wet_all[j] for j in range(span)]
        for step in range(STEPS):
            new = list(old)
            flux_up = face_rows[step] * (old[step + 1] - old[step])
            for j in range(step + 1, span - 1 - step):
                here = old[j]
                flux_down = face_rows[j] * (old[j + 1] - here)
                flux = face_cols[j] * (pltpu.roll(here, cols - 1, 1) - here)
                new[j] = here + (flux_down - flux_up) + (flux - pltpu.roll(flux, 1, 1))
                flux_up = flux_down
            old = new
        for r in range(kept):
            state[r, pl.ds(at, GROUP), :] = old[STEPS + r]
        return carry

    lax.fori_loop(0, groups, diffuse, 0)

    for r in range(kept):
        value = state[r]
        high = value.astype(jnp.bfloat16)
        low = (value - high.astype(jnp.float32)).astype(jnp.bfloat16)
        dot = functools.partial(jnp.dot, preferred_element_type=jnp.float32)
        mixed = dot(vert_hi, high) + (dot(vert_hi, low) + dot(vert_lo, high))
        if r < rows:
            scale = scale_ref[r : r + 1, :]
        else:
            scale = below_recv[rows : rows + 1, :]
        field[r * padded : (r + 1) * padded, :] = (mixed * scale).astype(jnp.bfloat16)

    def await_probe(k, carry):
        source = lax.rem(me + k, n)
        probe_copy(source, source).wait_recv()
        return carry

    lax.fori_loop(1, n, await_probe, 0)

    col_ids = lax.broadcasted_iota(jnp.int32, (cols, 2 * slots), 0).astype(jnp.float32)

    def answer(pair):
        probes = jnp.concatenate([probe_recv[2 * pair], probe_recv[2 * pair + 1]], 1)
        col, frac_x, row = probes[0:1], probes[1:2], probes[2:3]
        top, bottom = probes[3:4], probes[4:5]
        weights = jnp.where(
            col_ids == col, 1.0 - frac_x, jnp.where(col_ids == col + 1.0, frac_x, 0.0)
        ).astype(jnp.bfloat16)
        across = jnp.dot(field[...], weights, preferred_element_type=jnp.float32)
        total = None
        for r in range(kept):
            share = jnp.where(row == float(r), top, jnp.where(row == float(r - 1), bottom, 0.0))
            term = across[r * padded : (r + 1) * padded] * share
            total = term if total is None else total + term
        total = total.astype(jnp.bfloat16)
        prof_send[2 * pair] = total[:, 0:slots]
        prof_send[2 * pair + 1] = total[:, slots : 2 * slots]

    def prof_copy(peer, slot):
        return pltpu.make_async_remote_copy(
            src_ref=prof_send.at[peer],
            dst_ref=prof_recv.at[slot],
            send_sem=prof_ss.at[peer],
            recv_sem=prof_rs.at[slot],
            device_id={"tile": peer},
            device_id_type=MESH,
        )

    pairs = n // 2
    my_pair = me // 2

    def answer_other(k, carry):
        pair = lax.rem(my_pair + k, pairs)
        answer(pair)
        prof_copy(2 * pair, me).start()
        prof_copy(2 * pair + 1, me).start()
        return carry

    lax.fori_loop(1, pairs, answer_other, 0)
    answer(my_pair)
    prof_copy(4 * my_pair + 1 - me, me).start()
    prof_ref[0, me] = prof_send[me, 0:levels, :]

    for r in range(rows):
        field_rows[:, r, :] = field[r * padded : (r + 1) * padded, :].astype(jnp.float32)
    pert_ref[...] = field_rows[0:levels].astype(jnp.bfloat16)

    def finish(k, carry):
        source = lax.rem(me + n - k, n)
        prof_copy(source, source).wait_recv()
        prof_ref[0, source] = prof_recv[source, 0:levels, :]
        return carry

    lax.fori_loop(1, n, finish, 0)

    def settle(k, carry):
        peer = lax.rem(me + k, n)
        probe_copy(peer, me).wait_send()
        prof_copy(peer, me).wait_send()
        return carry

    lax.fori_loop(1, n, settle, 0)
    for which in range(3):
        edge_copy(which).wait_send()


def body(
    noise_seeds, diffusivity, wet_mask, vert_factor, norm_scale, obs_cell, obs_frac, obs_count
):
    rows, cols = diffusivity.shape
    levels = vert_factor.shape[0]
    n = lax.axis_size("tile")
    slots = obs_cell.shape[2]
    if rows != STEPS or n % 2 or cols & (cols - 1):
        raise ValueError("unsupported sizes")
    padded = -(-levels // 16) * 16
    span = rows + 2 * STEPS + 1
    kept = rows + 1
    f32, bf16 = jnp.float32, jnp.bfloat16
    vmem = pl.BlockSpec(memory_space=pltpu.VMEM)
    hbm = pl.BlockSpec(memory_space=pltpu.HBM)
    dma = pltpu.SemaphoreType.DMA
    return pl.pallas_call(
        functools.partial(kernel, n),
        out_shape=(
            jax.ShapeDtypeStruct((levels, rows, cols), bf16),
            jax.ShapeDtypeStruct((1, n, levels, slots), bf16),
        ),
        in_specs=[hbm] * 8,
        out_specs=(vmem, vmem),
        scratch_shapes=[
            pltpu.SMEM(noise_seeds.shape, jnp.int32),
            pltpu.SMEM(obs_count.shape, jnp.int32),
            pltpu.VMEM(diffusivity.shape, f32),
            pltpu.VMEM(wet_mask.shape, jnp.int32),
            pltpu.VMEM(vert_factor.shape, f32),
            pltpu.VMEM(norm_scale.shape, f32),
            pltpu.VMEM(obs_cell.shape, jnp.int32),
            pltpu.VMEM(obs_frac.shape, f32),
            dma((8,)),
            pltpu.VMEM((2 * rows, cols), f32),
            pltpu.VMEM((rows, cols), f32),
            pltpu.VMEM((2 * rows, cols), f32),
            pltpu.VMEM((rows, cols), f32),
            pltpu.VMEM((n, 8, slots), f32),
            pltpu.VMEM((n, 8, slots), f32),
            pltpu.VMEM((span, padded, cols), f32),
            pltpu.VMEM((span, GROUP, cols), f32),
            pltpu.VMEM((span, GROUP, cols), f32),
            pltpu.VMEM((span, GROUP, cols), f32),
            pltpu.VMEM((kept, padded, cols), f32),
            pltpu.VMEM((padded, 128), f32),
            pltpu.VMEM((kept * padded, cols), bf16),
            pltpu.VMEM((padded, rows, cols), f32),
            pltpu.VMEM((n, padded, slots), bf16),
            pltpu.VMEM((n, padded, slots), bf16),
            dma((3,)),
            dma((3,)),
            dma((n,)),
            dma((n,)),
            dma((n,)),
            dma((n,)),
        ],
        compiler_params=pltpu.CompilerParams(
            collective_id=0, has_side_effects=True, vmem_limit_bytes=60 * 1024 * 1024
        ),
    )(
        noise_seeds,
        obs_count,
        diffusivity,
        wet_mask,
        vert_factor,
        norm_scale,
        obs_cell,
        obs_frac,
    )


def solution(mesh):
    in_specs = (
        P("member"),
        P("tile", None),
        P("tile", None),
        P(),
        P("tile", None),
        P("tile", None, None),
        P("tile", None, None, None),
        P("tile", None),
    )
    out_specs = (P("member", "tile", None), P("tile", None, "member", None))
    return jax.shard_map(body, mesh=mesh, in_specs=in_specs, out_specs=out_specs, check_vma=False)
```

```python
import functools

import jax
import jax.numpy as jnp
from jax import lax
from jax.experimental import pallas as pl
from jax.experimental.pallas import tpu as pltpu
from jax.sharding import PartitionSpec as P

STEPS = 8
GROUP = 8
SPREAD = 3.4641016151377544
MESH = pl.DeviceIdType.MESH


def scramble(hashed):
    hashed = (hashed ^ lax.shift_right_logical(hashed, jnp.int32(16))) * jnp.int32(-2048144789)
    hashed = (hashed ^ lax.shift_right_logical(hashed, jnp.int32(13))) * jnp.int32(-1028477387)
    return hashed ^ lax.shift_right_logical(hashed, jnp.int32(16))


def kernel(
    n,
    seeds_hbm,
    count_hbm,
    diff_hbm,
    wet_hbm,
    vert_hbm,
    scale_hbm,
    cell_hbm,
    frac_hbm,
    pert_ref,
    prof_ref,
    seeds_ref,
    count_ref,
    diff_ref,
    wet_ref,
    vert_ref,
    scale_ref,
    cell_ref,
    frac_ref,
    in_sems,
    edge_send,
    above_recv,
    below_recv,
    next_recv,
    probe_send,
    probe_recv,
    noise,
    face_rows,
    face_cols,
    wet_all,
    scale_all,
    state,
    vert_pad,
    scaled,
    weights,
    shares,
    field,
    field_rows,
    prof_rows,
    prof_send,
    prof_recv,
    edge_ss,
    edge_rs,
    probe_ss,
    probe_rs,
    prof_ss,
    prof_rs,
):
    pulls = [
        pltpu.make_async_copy(src, dst, in_sems.at[k])
        for k, (src, dst) in enumerate(
            (
                (diff_hbm, diff_ref),
                (wet_hbm, wet_ref),
                (scale_hbm, scale_ref),
                (seeds_hbm, seeds_ref),
                (count_hbm, count_ref),
                (cell_hbm, cell_ref),
                (frac_hbm, frac_ref),
                (vert_hbm, vert_ref),
            )
        )
    ]
    for pull in pulls:
        pull.start()

    me = lax.axis_index("tile")
    rows, cols = diff_ref.shape
    half = cols // 2
    levels = vert_ref.shape[0]
    padded = state.shape[1]
    groups = padded // GROUP
    slots = cell_ref.shape[2]
    total_rows = n * rows
    span = rows + 2 * STEPS + 1
    kept = rows + 1

    barrier = pltpu.get_barrier_semaphore()

    def greet(k, carry):
        peer = lax.rem(me + k, n)
        pl.semaphore_signal(barrier, inc=1, device_id={"tile": peer}, device_id_type=MESH)
        return carry

    lax.fori_loop(1, n, greet, 0)

    for pull in pulls:
        pull.wait()

    kappa = diff_ref[...] * wet_ref[...].astype(jnp.float32)
    pair_shape = (cols, cols)
    lane = lax.broadcasted_iota(jnp.int32, pair_shape, 1)
    lane = jnp.where(lane < half, 2 * lane, 2 * lane - (cols - 1))
    split = jnp.where(lax.broadcasted_iota(jnp.int32, pair_shape, 0) == lane, 1.0, 0.0)
    edge_send[...] = jnp.dot(
        jnp.concatenate([kappa, scale_ref[...]], 0),
        split,
        precision=lax.Precision.HIGHEST,
        preferred_element_type=jnp.float32,
    )
    slot_ids = lax.broadcasted_iota(jnp.int32, (1, slots), 1)

    def pack(h, carry):
        anchor = cell_ref[0, pl.ds(h, 1), :]
        frac = frac_ref[0, h]
        row = lax.shift_right_logical(anchor, jnp.int32(cols.bit_length() - 1))
        col = anchor - row * cols
        probe_send[h, 0:1, :] = col.astype(jnp.float32)
        probe_send[h, 1:2, :] = frac[1:2, :]
        probe_send[h, 2:3, :] = row.astype(jnp.float32)
        probe_send[h, 3:4, :] = frac[0:1, :]
        probe_send[h, 4:8, :] = jnp.zeros((4, slots), jnp.float32)
        return carry

    lax.fori_loop(0, n, pack, 0)

    seed_a = seeds_ref[0]
    seed_b = seeds_ref[1]
    shape = (GROUP, cols)
    col_ids = lax.broadcasted_iota(jnp.int32, shape, 1)
    col_ids = jnp.where(col_ids < half, 2 * col_ids, 2 * col_ids - (cols - 1))
    spread_ids = (
        lax.broadcasted_iota(jnp.int32, shape, 0) * (total_rows * cols) + col_ids
    ) * jnp.int32(-1640531535)
    first_row = me * rows - STEPS

    def draw(g, carry):
        at = pl.multiple_of(g * GROUP, GROUP)
        for j in range(span):
            base = (g * (GROUP * total_rows) + first_row + j) * cols
            hashed = scramble(spread_ids + (base * jnp.int32(-1640531535) + seed_a))
            hashed = scramble(hashed ^ seed_b)
            drawn = lax.shift_right_logical(hashed, jnp.int32(8)).astype(jnp.float32)
            noise[j, pl.ds(at, GROUP), :] = drawn * (SPREAD / 16777216.0) + SPREAD * (
                0.5 / 16777216.0 - 0.5
            )
        return carry

    lax.fori_loop(0, groups // 2, draw, 0)

    pl.semaphore_wait(barrier, n - 1)

    def edge_copy(which):
        if which == 0:
            src, dst, by = edge_send.at[pl.ds(0, rows)], above_recv, 1
        elif which == 1:
            src, dst, by = edge_send, below_recv, n - 1
        else:
            src, dst, by = edge_send.at[pl.ds(0, rows)], next_recv, n - 2
        return pltpu.make_async_remote_copy(
            src_ref=src,
            dst_ref=dst,
            send_sem=edge_ss.at[which],
            recv_sem=edge_rs.at[which],
            device_id={"tile": lax.rem(me + by, n)},
            device_id_type=MESH,
        )

    def probe_copy(peer, slot):
        return pltpu.make_async_remote_copy(
            src_ref=probe_send.at[peer],
            dst_ref=probe_recv.at[slot],
            send_sem=probe_ss.at[peer],
            recv_sem=probe_rs.at[slot],
            device_id={"tile": peer},
            device_id_type=MESH,
        )

    for which in range(3):
        edge_copy(which).start()

    def send_probe(k, carry):
        probe_copy(lax.rem(me + k, n), me).start()
        return carry

    lax.fori_loop(1, n, send_probe, 0)
    probe_recv[me] = probe_send[me]

    lax.fori_loop(groups // 2, groups, draw, 0)

    vert_pad[...] = jnp.zeros_like(vert_pad)
    vert_pad[0:levels, 0:levels] = vert_ref[...]
    vert = vert_pad[:, 0:padded]
    vert_hi = vert.astype(jnp.bfloat16)
    vert_lo = (vert - vert_hi.astype(jnp.float32)).astype(jnp.bfloat16)

    for which in range(3):
        edge_copy(which).wait_recv()

    zero = jnp.zeros((rows, cols), jnp.float32)
    kappa_all = jnp.concatenate(
        [
            jnp.where(me > 0, above_recv[...], zero),
            edge_send[0:rows, :],
            jnp.where(me < n - 1, below_recv[0:rows, :], zero),
            jnp.where(me < n - 2, next_recv[...], zero),
        ],
        0,
    )
    wet = jnp.where(kappa_all > 0.0, 1.0, 0.0)
    even, odd = kappa_all[:, 0:half], kappa_all[:, half:cols]
    last = lax.broadcasted_iota(jnp.int32, even.shape, 1) == half - 1
    faces_in = jnp.sqrt(even * odd)
    faces_out = jnp.where(last, 0.0, jnp.sqrt(odd * pltpu.roll(even, half - 1, 1)))
    faces_c = jnp.concatenate([faces_in, faces_out], 1)
    faces_r = jnp.sqrt(kappa_all[0 : span - 1] * kappa_all[1:span])
    for j in range(span):
        wet_all[j] = jnp.broadcast_to(wet[j : j + 1], shape)
        face_cols[j] = jnp.broadcast_to(faces_c[j : j + 1], shape)
        if j < span - 1:
            face_rows[j] = jnp.broadcast_to(faces_r[j : j + 1], shape)
    for r in range(kept):
        row = edge_send[rows + r : rows + r + 1] if r < rows else below_recv[rows : rows + 1]
        scale_all[r] = jnp.broadcast_to(row, shape)

    def await_probe(k, carry):
        source = lax.rem(me + k, n)
        probe_copy(source, source).wait_recv()
        return carry

    lax.fori_loop(1, n, await_probe, 0)

    pairs = n // 2
    cell_ids = lax.broadcasted_iota(jnp.int32, (cols, 2 * slots), 0)
    cell_ids = jnp.where(cell_ids < half, 2 * cell_ids, 2 * cell_ids - (cols - 1))
    cell_ids = cell_ids.astype(jnp.float32)

    def weigh(pair, carry):
        probes = jnp.concatenate([probe_recv[2 * pair], probe_recv[2 * pair + 1]], 1)
        col, frac_x, row, frac_y = probes[0:1], probes[1:2], probes[2:3], probes[3:4]
        weights[pair] = jnp.where(
            cell_ids == col, 1.0 - frac_x, jnp.where(cell_ids == col + 1.0, frac_x, 0.0)
        ).astype(jnp.bfloat16)
        for r in range(kept):
            shares[pair, r : r + 1, :] = jnp.where(
                row == float(r), 1.0 - frac_y, jnp.where(row == float(r - 1), frac_y, 0.0)
            )
        return carry

    lax.fori_loop(0, pairs, weigh, 0)

    def advance(at):
        def take(ref, j, lo):
            return ref[j, :, lo : lo + half]

        old_e, old_o = [], []
        for j in range(span):
            old_e.append(noise[j, pl.ds(at, GROUP), 0:half] * take(wet_all, j, 0))
            old_o.append(noise[j, pl.ds(at, GROUP), half:cols] * take(wet_all, j, half))
        for step in range(STEPS):
            new_e, new_o = list(old_e), list(old_o)
            up_e = take(face_rows, step, 0) * (old_e[step + 1] - old_e[step])
            up_o = take(face_rows, step, half) * (old_o[step + 1] - old_o[step])
            for j in range(step + 1, span - 1 - step):
                here_e, here_o = old_e[j], old_o[j]
                down_e = take(face_rows, j, 0) * (old_e[j + 1] - here_e)
                down_o = take(face_rows, j, half) * (old_o[j + 1] - here_o)
                inner = take(face_cols, j, 0) * (here_o - here_e)
                outer = take(face_cols, j, half) * (pltpu.roll(here_e, half - 1, 1) - here_o)
                new_e[j] = here_e + ((down_e - up_e) + (inner - pltpu.roll(outer, 1, 1)))
                new_o[j] = here_o + ((down_o - up_o) + (outer - inner))
                up_e, up_o = down_e, down_o
            old_e, old_o = new_e, new_o
        return old_e[STEPS : STEPS + kept], old_o[STEPS : STEPS + kept]

    def prof_copy(peer, slot, at, size):
        return pltpu.make_async_remote_copy(
            src_ref=prof_send.at[peer, pl.ds(at, size)],
            dst_ref=prof_recv.at[slot, pl.ds(at, size)],
            send_sem=prof_ss.at[peer],
            recv_sem=prof_rs.at[slot],
            device_id={"tile": peer},
            device_id_type=MESH,
        )

    block = 2 * GROUP
    my_pair = me // 2

    def turn(b, carry):
        first = pl.multiple_of(b * block, block)
        for part in range(2):
            at = pl.multiple_of(first + part * GROUP, GROUP)
            evens, odds = advance(at)
            for r in range(kept):
                if r < rows:
                    state[r, pl.ds(at, GROUP), 0:half] = evens[r]
                    state[r, pl.ds(at, GROUP), half:cols] = odds[r]
                line = r * block + part * GROUP
                scaled[line : line + GROUP, 0:half] = evens[r] * scale_all[r, :, 0:half]
                scaled[line : line + GROUP, half:cols] = odds[r] * scale_all[r, :, half:cols]
        left = scaled[...].astype(jnp.bfloat16)

        def answer(pair):
            across = jnp.dot(left, weights[pair], preferred_element_type=jnp.float32)
            total = None
            for r in range(kept):
                term = across[r * block : (r + 1) * block] * shares[pair, r : r + 1, :]
                total = term if total is None else total + term
            total = total.astype(jnp.bfloat16)
            prof_send[2 * pair, pl.ds(first, block), :] = total[:, 0:slots]
            prof_send[2 * pair + 1, pl.ds(first, block), :] = total[:, slots : 2 * slots]

        for k in range(1, pairs + 1):
            answer(lax.rem(my_pair + k, pairs))

        def send(k, inner):
            prof_copy(lax.rem(2 * my_pair + 2 + k, n), me, first, block).start()
            return inner

        lax.fori_loop(0, n - 2, send, 0)
        prof_copy(4 * my_pair + 1 - me, me, first, block).start()
        return carry

    lax.fori_loop(0, padded // block, turn, 0)
    prof_recv[me] = prof_send[me]

    dot = functools.partial(jnp.dot, preferred_element_type=jnp.float32)
    for r in range(rows):
        value = state[r]
        high = value.astype(jnp.bfloat16)
        low = (value - high.astype(jnp.float32)).astype(jnp.bfloat16)
        mixed = dot(vert_hi, high) + (dot(vert_hi, low) + dot(vert_lo, high))
        scale = edge_send[rows + r : rows + r + 1, :]
        field[r * padded : (r + 1) * padded, :] = (mixed * scale).astype(jnp.bfloat16)
    lane = lax.broadcasted_iota(jnp.int32, pair_shape, 0)
    lane = jnp.where(lane < half, 2 * lane, 2 * lane - (cols - 1))
    merge = jnp.where(lax.broadcasted_iota(jnp.int32, pair_shape, 1) == lane, 1.0, 0.0)
    merge = merge.astype(jnp.bfloat16)
    for r in range(rows):
        field_rows[:, r, :] = dot(field[r * padded : (r + 1) * padded, :], merge)
    pert_ref[...] = field_rows[0:levels].astype(jnp.bfloat16)

    def await_prof(k, carry):
        source = lax.rem(me + n - k, n)
        prof_copy(source, source, 0, padded).wait_recv()
        return carry

    lax.fori_loop(1, n, await_prof, 0)

    both = jnp.concatenate([vert_hi, vert_lo], 0)
    for source in range(0, n, 2):
        arrived = jnp.concatenate([prof_recv[source], prof_recv[source + 1]], 1)
        mixed = dot(both, arrived)
        mixed = mixed[0:padded] + mixed[padded : 2 * padded]
        for side in range(2):
            live = slot_ids < count_ref[0, source + side]
            prof_rows[:, source + side, :] = jnp.where(
                live, mixed[:, side * slots : (side + 1) * slots], 0.0
            )
    prof_ref[...] = prof_rows[0:levels].astype(jnp.bfloat16)

    def settle(k, carry):
        peer = lax.rem(me + k, n)
        probe_copy(peer, me).wait_send()
        prof_copy(peer, me, 0, padded).wait_send()
        return carry

    lax.fori_loop(1, n, settle, 0)
    for which in range(3):
        edge_copy(which).wait_send()


def body(
    noise_seeds, diffusivity, wet_mask, vert_factor, norm_scale, obs_cell, obs_frac, obs_count
):
    rows, cols = diffusivity.shape
    levels = vert_factor.shape[0]
    n = lax.axis_size("tile")
    slots = obs_cell.shape[2]
    if rows != STEPS or n % 2 or cols & (cols - 1):
        raise ValueError("unsupported sizes")
    padded = -(-levels // 16) * 16
    span = rows + 2 * STEPS + 1
    kept = rows + 1
    f32, bf16 = jnp.float32, jnp.bfloat16
    vmem = pl.BlockSpec(memory_space=pltpu.VMEM)
    hbm = pl.BlockSpec(memory_space=pltpu.HBM)
    dma = pltpu.SemaphoreType.DMA
    perturbation, profiles = pl.pallas_call(
        functools.partial(kernel, n),
        out_shape=(
            jax.ShapeDtypeStruct((levels, rows, cols), bf16),
            jax.ShapeDtypeStruct((levels, n, slots), bf16),
        ),
        in_specs=[hbm] * 8,
        out_specs=(vmem, vmem),
        scratch_shapes=[
            pltpu.SMEM(noise_seeds.shape, jnp.int32),
            pltpu.SMEM(obs_count.shape, jnp.int32),
            pltpu.VMEM(diffusivity.shape, f32),
            pltpu.VMEM(wet_mask.shape, jnp.int32),
            pltpu.VMEM(vert_factor.shape, f32),
            pltpu.VMEM(norm_scale.shape, f32),
            pltpu.VMEM(obs_cell.shape, jnp.int32),
            pltpu.VMEM(obs_frac.shape, f32),
            dma((8,)),
            pltpu.VMEM((2 * rows, cols), f32),
            pltpu.VMEM((rows, cols), f32),
            pltpu.VMEM((2 * rows, cols), f32),
            pltpu.VMEM((rows, cols), f32),
            pltpu.VMEM((n, 8, slots), f32),
            pltpu.VMEM((n, 8, slots), f32),
            pltpu.VMEM((span, padded, cols), f32),
            pltpu.VMEM((span, GROUP, cols), f32),
            pltpu.VMEM((span, GROUP, cols), f32),
            pltpu.VMEM((span, GROUP, cols), f32),
            pltpu.VMEM((kept, GROUP, cols), f32),
            pltpu.VMEM((rows, padded, cols), f32),
            pltpu.VMEM((padded, 128), f32),
            pltpu.VMEM((kept * 2 * GROUP, cols), f32),
            pltpu.VMEM((n // 2, cols, 2 * slots), bf16),
            pltpu.VMEM((n // 2, 2 * GROUP, 2 * slots), f32),
            pltpu.VMEM((rows * padded, cols), bf16),
            pltpu.VMEM((padded, rows, cols), f32),
            pltpu.VMEM((padded, n, slots), f32),
            pltpu.VMEM((n, padded, slots), bf16),
            pltpu.VMEM((n, padded, slots), bf16),
            dma((3,)),
            dma((3,)),
            dma((n,)),
            dma((n,)),
            dma((n,)),
            dma((n,)),
        ],
        compiler_params=pltpu.CompilerParams(
            collective_id=0, has_side_effects=True, vmem_limit_bytes=60 * 1024 * 1024
        ),
    )(
        noise_seeds,
        obs_count,
        diffusivity,
        wet_mask,
        vert_factor,
        norm_scale,
        obs_cell,
        obs_frac,
    )
    return (perturbation, jnp.transpose(profiles, (1, 0, 2))[None])


def solution(mesh):
    in_specs = (
        P("member"),
        P("tile", None),
        P("tile", None),
        P(),
        P("tile", None),
        P("tile", None, None),
        P("tile", None, None, None),
        P("tile", None),
    )
    out_specs = (P("member", "tile", None), P("tile", None, "member", None))
    return jax.shard_map(body, mesh=mesh, in_specs=in_specs, out_specs=out_specs, check_vma=False)
```

```python
import functools

import jax
import jax.numpy as jnp
from jax import lax
from jax.experimental import pallas as pl
from jax.experimental.pallas import tpu as pltpu
from jax.sharding import PartitionSpec as P

STEPS = 8
GROUP = 8
SPREAD = 3.4641016151377544
MESH = pl.DeviceIdType.MESH


def scramble(hashed):
    hashed = (hashed ^ lax.shift_right_logical(hashed, jnp.int32(16))) * jnp.int32(-2048144789)
    hashed = (hashed ^ lax.shift_right_logical(hashed, jnp.int32(13))) * jnp.int32(-1028477387)
    return hashed ^ lax.shift_right_logical(hashed, jnp.int32(16))


def kernel(
    n,
    seeds_hbm,
    count_hbm,
    diff_hbm,
    wet_hbm,
    vert_hbm,
    scale_hbm,
    cell_hbm,
    frac_hbm,
    pert_ref,
    prof_ref,
    seeds_ref,
    count_ref,
    diff_ref,
    wet_ref,
    vert_ref,
    scale_ref,
    cell_ref,
    frac_ref,
    in_sems,
    edge_send,
    above_recv,
    below_recv,
    next_recv,
    probe_send,
    probe_recv,
    noise,
    face_rows,
    face_cols,
    wet_all,
    scale_all,
    state,
    vert_pad,
    scaled,
    weights,
    shares,
    field,
    field_rows,
    prof_send,
    prof_recv,
    edge_ss,
    edge_rs,
    probe_ss,
    probe_rs,
    prof_ss,
    prof_rs,
):
    pulls = [
        pltpu.make_async_copy(src, dst, in_sems.at[k])
        for k, (src, dst) in enumerate(
            (
                (diff_hbm, diff_ref),
                (wet_hbm, wet_ref),
                (scale_hbm, scale_ref),
                (seeds_hbm, seeds_ref),
                (count_hbm, count_ref),
                (cell_hbm, cell_ref),
                (frac_hbm, frac_ref),
                (vert_hbm, vert_ref),
            )
        )
    ]
    for pull in pulls:
        pull.start()

    me = lax.axis_index("tile")
    rows, cols = diff_ref.shape
    half = cols // 2
    levels = vert_ref.shape[0]
    padded = state.shape[1]
    groups = padded // GROUP
    slots = cell_ref.shape[2]
    total_rows = n * rows
    span = rows + 2 * STEPS + 1
    kept = rows + 1

    barrier = pltpu.get_barrier_semaphore()

    def greet(k, carry):
        peer = lax.rem(me + k, n)
        pl.semaphore_signal(barrier, inc=1, device_id={"tile": peer}, device_id_type=MESH)
        return carry

    lax.fori_loop(1, n, greet, 0)

    for pull in pulls:
        pull.wait()

    kappa = diff_ref[...] * wet_ref[...].astype(jnp.float32)
    dot = functools.partial(jnp.dot, preferred_element_type=jnp.float32)
    pair_shape = (cols, cols)
    lane = lax.broadcasted_iota(jnp.int32, pair_shape, 1)
    lane = jnp.where(lane < half, 2 * lane, 2 * lane - (cols - 1))
    split = jnp.where(lax.broadcasted_iota(jnp.int32, pair_shape, 0) == lane, 1.0, 0.0)
    plain = jnp.concatenate([kappa, scale_ref[...]], 0)
    high = plain.astype(jnp.bfloat16)
    rest = plain - high.astype(jnp.float32)
    middle = rest.astype(jnp.bfloat16)
    low = (rest - middle.astype(jnp.float32)).astype(jnp.bfloat16)
    terms = dot(jnp.concatenate([high, middle, low], 0), split.astype(jnp.bfloat16))
    edge_send[...] = (terms[0 : 2 * rows] + terms[2 * rows : 4 * rows]) + terms[4 * rows :]

    pl.semaphore_wait(barrier, n - 1)

    def edge_copy(which):
        if which == 0:
            src, dst, by = edge_send.at[pl.ds(0, rows)], above_recv, 1
        elif which == 1:
            src, dst, by = edge_send, below_recv, n - 1
        else:
            src, dst, by = edge_send.at[pl.ds(0, rows)], next_recv, n - 2
        return pltpu.make_async_remote_copy(
            src_ref=src,
            dst_ref=dst,
            send_sem=edge_ss.at[which],
            recv_sem=edge_rs.at[which],
            device_id={"tile": lax.rem(me + by, n)},
            device_id_type=MESH,
        )

    def probe_copy(peer, slot):
        return pltpu.make_async_remote_copy(
            src_ref=probe_send.at[peer],
            dst_ref=probe_recv.at[slot],
            send_sem=probe_ss.at[peer],
            recv_sem=probe_rs.at[slot],
            device_id={"tile": peer},
            device_id_type=MESH,
        )

    for which in range(3):
        edge_copy(which).start()

    slot_ids = lax.broadcasted_iota(jnp.int32, (1, slots), 1)

    def pack(h, carry):
        anchor = cell_ref[0, pl.ds(h, 1), :]
        frac = frac_ref[0, h]
        row = lax.shift_right_logical(anchor, jnp.int32(cols.bit_length() - 1))
        col = anchor - row * cols
        probe_send[h, 0:1, :] = col.astype(jnp.float32)
        probe_send[h, 1:2, :] = frac[1:2, :]
        probe_send[h, 2:3, :] = row.astype(jnp.float32)
        probe_send[h, 3:4, :] = frac[0:1, :]
        probe_send[h, 4:8, :] = jnp.zeros((4, slots), jnp.float32)
        return carry

    lax.fori_loop(0, n, pack, 0)

    def send_probe(k, carry):
        probe_copy(lax.rem(me + k, n), me).start()
        return carry

    lax.fori_loop(1, n, send_probe, 0)
    probe_recv[me] = probe_send[me]

    seed_a = seeds_ref[0]
    seed_b = seeds_ref[1]
    shape = (GROUP, cols)
    col_ids = lax.broadcasted_iota(jnp.int32, shape, 1)
    col_ids = jnp.where(col_ids < half, 2 * col_ids, 2 * col_ids - (cols - 1))
    spread_ids = (
        lax.broadcasted_iota(jnp.int32, shape, 0) * (total_rows * cols) + col_ids
    ) * jnp.int32(-1640531535)
    first_row = me * rows - STEPS

    def draw(g, carry):
        at = pl.multiple_of(g * GROUP, GROUP)
        for j in range(span):
            base = (g * (GROUP * total_rows) + first_row + j) * cols
            hashed = scramble(spread_ids + (base * jnp.int32(-1640531535) + seed_a))
            hashed = scramble(hashed ^ seed_b)
            drawn = lax.shift_right_logical(hashed, jnp.int32(8)).astype(jnp.float32)
            noise[j, pl.ds(at, GROUP), :] = drawn * (SPREAD / 16777216.0) + SPREAD * (
                0.5 / 16777216.0 - 0.5
            )
        return carry

    lax.fori_loop(0, groups, draw, 0)

    vert_pad[...] = jnp.zeros_like(vert_pad)
    vert_pad[0:levels, 0:levels] = vert_ref[...]
    vert = vert_pad[:, 0:padded]
    vert_hi = vert.astype(jnp.bfloat16)
    vert_lo = (vert - vert_hi.astype(jnp.float32)).astype(jnp.bfloat16)

    for which in range(3):
        edge_copy(which).wait_recv()

    zero = jnp.zeros((rows, cols), jnp.float32)
    kappa_all = jnp.concatenate(
        [
            jnp.where(me > 0, above_recv[...], zero),
            edge_send[0:rows, :],
            jnp.where(me < n - 1, below_recv[0:rows, :], zero),
            jnp.where(me < n - 2, next_recv[...], zero),
        ],
        0,
    )
    wet = jnp.where(kappa_all > 0.0, 1.0, 0.0)
    even, odd = kappa_all[:, 0:half], kappa_all[:, half:cols]
    last = lax.broadcasted_iota(jnp.int32, even.shape, 1) == half - 1
    faces_in = jnp.sqrt(even * odd)
    faces_out = jnp.where(last, 0.0, jnp.sqrt(odd * pltpu.roll(even, half - 1, 1)))
    faces_c = jnp.concatenate([faces_in, faces_out], 1)
    faces_r = jnp.sqrt(kappa_all[0 : span - 1] * kappa_all[1:span])
    for j in range(span):
        wet_all[j] = jnp.broadcast_to(wet[j : j + 1], shape)
        face_cols[j] = jnp.broadcast_to(faces_c[j : j + 1], shape)
        if j < span - 1:
            face_rows[j] = jnp.broadcast_to(faces_r[j : j + 1], shape)
    for r in range(kept):
        row = edge_send[rows + r : rows + r + 1] if r < rows else below_recv[rows : rows + 1]
        scale_all[r] = jnp.broadcast_to(row, shape)

    def await_probe(k, carry):
        source = lax.rem(me + k, n)
        probe_copy(source, source).wait_recv()
        return carry

    lax.fori_loop(1, n, await_probe, 0)

    pairs = n // 2
    cell_ids = lax.broadcasted_iota(jnp.int32, (cols, 2 * slots), 0)
    cell_ids = jnp.where(cell_ids < half, 2 * cell_ids, 2 * cell_ids - (cols - 1))
    cell_ids = cell_ids.astype(jnp.float32)

    def weigh(pair, carry):
        probes = jnp.concatenate([probe_recv[2 * pair], probe_recv[2 * pair + 1]], 1)
        col, frac_x, row, frac_y = probes[0:1], probes[1:2], probes[2:3], probes[3:4]
        weights[pair] = jnp.where(
            cell_ids == col, 1.0 - frac_x, jnp.where(cell_ids == col + 1.0, frac_x, 0.0)
        ).astype(jnp.bfloat16)
        for r in range(kept):
            shares[pair, r : r + 1, :] = jnp.where(
                row == float(r), 1.0 - frac_y, jnp.where(row == float(r - 1), frac_y, 0.0)
            )
        return carry

    lax.fori_loop(0, pairs, weigh, 0)

    def advance(at):
        def take(ref, j, lo):
            return ref[j, :, lo : lo + half]

        old_e, old_o = [], []
        for j in range(span):
            old_e.append(noise[j, pl.ds(at, GROUP), 0:half] * take(wet_all, j, 0))
            old_o.append(noise[j, pl.ds(at, GROUP), half:cols] * take(wet_all, j, half))
        for step in range(STEPS):
            new_e, new_o = list(old_e), list(old_o)
            up_e = take(face_rows, step, 0) * (old_e[step + 1] - old_e[step])
            up_o = take(face_rows, step, half) * (old_o[step + 1] - old_o[step])
            for j in range(step + 1, span - 1 - step):
                here_e, here_o = old_e[j], old_o[j]
                down_e = take(face_rows, j, 0) * (old_e[j + 1] - here_e)
                down_o = take(face_rows, j, half) * (old_o[j + 1] - here_o)
                inner = take(face_cols, j, 0) * (here_o - here_e)
                outer = take(face_cols, j, half) * (pltpu.roll(here_e, half - 1, 1) - here_o)
                new_e[j] = here_e + ((down_e - up_e) + (inner - pltpu.roll(outer, 1, 1)))
                new_o[j] = here_o + ((down_o - up_o) + (outer - inner))
                up_e, up_o = down_e, down_o
            old_e, old_o = new_e, new_o
        return old_e[STEPS : STEPS + kept], old_o[STEPS : STEPS + kept]

    def prof_copy(peer, slot, at, size):
        return pltpu.make_async_remote_copy(
            src_ref=prof_send.at[peer, pl.ds(at, size)],
            dst_ref=prof_recv.at[slot, pl.ds(at, size)],
            send_sem=prof_ss.at[peer],
            recv_sem=prof_rs.at[slot],
            device_id={"tile": peer},
            device_id_type=MESH,
        )

    block = 2 * GROUP
    my_pair = me // 2
    some = pairs // 2

    def answer(left, first, side):
        for q in range(some):
            pair = lax.rem(my_pair + 1 + side * some + q, pairs)
            across = dot(left, weights[pair])
            total = None
            for r in range(kept):
                term = across[r * block : (r + 1) * block] * shares[pair, r : r + 1, :]
                total = term if total is None else total + term
            total = total.astype(jnp.bfloat16)
            prof_send[2 * pair, pl.ds(first, block), :] = total[:, 0:slots]
            prof_send[2 * pair + 1, pl.ds(first, block), :] = total[:, slots : 2 * slots]

    def send(ready, first, side):
        for k in range(2 * some):
            peer = lax.rem(2 * (my_pair + 1 + side * some) + k, n)

            @pl.when(jnp.logical_and(ready, peer != me))
            def _():
                prof_copy(peer, me, first, block).start()

    def left_of(slot):
        return scaled[slot].reshape(kept * block, cols).astype(jnp.bfloat16)

    def turn(g, carry):
        at = pl.multiple_of(g * GROUP, GROUP)
        side = lax.rem(g, 2)
        slot = lax.rem(g // 2, 2)
        before = pl.multiple_of(jnp.maximum(g // 2 - 1, 0) * block, block)
        answer(left_of(1 - slot), before, side)
        evens, odds = advance(at)
        line = pl.multiple_of(side * GROUP, GROUP)
        for r in range(kept):
            if r < rows:
                state[r, pl.ds(at, GROUP), 0:half] = evens[r]
                state[r, pl.ds(at, GROUP), half:cols] = odds[r]
            scaled[slot, r, pl.ds(line, GROUP), 0:half] = evens[r] * scale_all[r, :, 0:half]
            scaled[slot, r, pl.ds(line, GROUP), half:cols] = (
                odds[r] * scale_all[r, :, half:cols]
            )
        send(g >= 2, before, side)
        return carry

    scaled[1] = jnp.zeros((kept, block, cols), jnp.float32)
    lax.fori_loop(0, groups, turn, 0)

    def last_turn(side, carry):
        answer(left_of((groups // 2 - 1) % 2), padded - block, side)
        send(side >= 0, padded - block, side)
        return carry

    lax.fori_loop(0, 2, last_turn, 0)
    prof_recv[me] = prof_send[me]

    for r in range(rows):
        value = state[r]
        high = value.astype(jnp.bfloat16)
        low = (value - high.astype(jnp.float32)).astype(jnp.bfloat16)
        mixed = dot(vert_hi, high) + (dot(vert_hi, low) + dot(vert_lo, high))
        scale = edge_send[rows + r : rows + r + 1, :]
        field[r * padded : (r + 1) * padded, :] = (mixed * scale).astype(jnp.bfloat16)
    lane = lax.broadcasted_iota(jnp.int32, pair_shape, 0)
    lane = jnp.where(lane < half, 2 * lane, 2 * lane - (cols - 1))
    merge = jnp.where(lax.broadcasted_iota(jnp.int32, pair_shape, 1) == lane, 1.0, 0.0)
    merge = merge.astype(jnp.bfloat16)
    for r in range(rows):
        field_rows[:, r, :] = dot(field[r * padded : (r + 1) * padded, :], merge)
    pert_ref[...] = field_rows[0:levels].astype(jnp.bfloat16)

    def await_prof(k, carry):
        source = lax.rem(me + n - k, n)
        prof_copy(source, source, 0, padded).wait_recv()
        return carry

    lax.fori_loop(1, n, await_prof, 0)

    both = jnp.concatenate([vert_hi, vert_lo], 0)
    for source in range(0, n, 2):
        arrived = jnp.concatenate([prof_recv[source], prof_recv[source + 1]], 1)
        mixed = dot(both, arrived)
        mixed = mixed[0:padded] + mixed[padded : 2 * padded]
        for side in range(2):
            live = slot_ids < count_ref[0, source + side]
            mine = mixed[0:levels, side * slots : (side + 1) * slots]
            prof_ref[0, source + side] = jnp.where(live, mine, 0.0).astype(jnp.bfloat16)

    def settle(k, carry):
        peer = lax.rem(me + k, n)
        probe_copy(peer, me).wait_send()
        prof_copy(peer, me, 0, padded).wait_send()
        return carry

    lax.fori_loop(1, n, settle, 0)
    for which in range(3):
        edge_copy(which).wait_send()


def body(
    noise_seeds, diffusivity, wet_mask, vert_factor, norm_scale, obs_cell, obs_frac, obs_count
):
    rows, cols = diffusivity.shape
    levels = vert_factor.shape[0]
    n = lax.axis_size("tile")
    slots = obs_cell.shape[2]
    if rows != STEPS or n % 4 or cols & (cols - 1):
        raise ValueError("unsupported sizes")
    padded = -(-levels // 16) * 16
    span = rows + 2 * STEPS + 1
    kept = rows + 1
    f32, bf16 = jnp.float32, jnp.bfloat16
    vmem = pl.BlockSpec(memory_space=pltpu.VMEM)
    hbm = pl.BlockSpec(memory_space=pltpu.HBM)
    dma = pltpu.SemaphoreType.DMA
    return pl.pallas_call(
        functools.partial(kernel, n),
        out_shape=(
            jax.ShapeDtypeStruct((levels, rows, cols), bf16),
            jax.ShapeDtypeStruct((1, n, levels, slots), bf16),
        ),
        in_specs=[hbm] * 8,
        out_specs=(vmem, vmem),
        scratch_shapes=[
            pltpu.SMEM(noise_seeds.shape, jnp.int32),
            pltpu.SMEM(obs_count.shape, jnp.int32),
            pltpu.VMEM(diffusivity.shape, f32),
            pltpu.VMEM(wet_mask.shape, jnp.int32),
            pltpu.VMEM(vert_factor.shape, f32),
            pltpu.VMEM(norm_scale.shape, f32),
            pltpu.VMEM(obs_cell.shape, jnp.int32),
            pltpu.VMEM(obs_frac.shape, f32),
            dma((8,)),
            pltpu.VMEM((2 * rows, cols), f32),
            pltpu.VMEM((rows, cols), f32),
            pltpu.VMEM((2 * rows, cols), f32),
            pltpu.VMEM((rows, cols), f32),
            pltpu.VMEM((n, 8, slots), f32),
            pltpu.VMEM((n, 8, slots), f32),
            pltpu.VMEM((span, padded, cols), f32),
            pltpu.VMEM((span, GROUP, cols), f32),
            pltpu.VMEM((span, GROUP, cols), f32),
            pltpu.VMEM((span, GROUP, cols), f32),
            pltpu.VMEM((kept, GROUP, cols), f32),
            pltpu.VMEM((rows, padded, cols), f32),
            pltpu.VMEM((padded, 128), f32),
            pltpu.VMEM((2, kept, 2 * GROUP, cols), f32),
            pltpu.VMEM((n // 2, cols, 2 * slots), bf16),
            pltpu.VMEM((n // 2, 2 * GROUP, 2 * slots), f32),
            pltpu.VMEM((rows * padded, cols), bf16),
            pltpu.VMEM((padded, rows, cols), f32),
            pltpu.VMEM((n, padded, slots), bf16),
            pltpu.VMEM((n, padded, slots), bf16),
            dma((3,)),
            dma((3,)),
            dma((n,)),
            dma((n,)),
            dma((n,)),
            dma((n,)),
        ],
        compiler_params=pltpu.CompilerParams(
            collective_id=0, has_side_effects=True, vmem_limit_bytes=60 * 1024 * 1024
        ),
    )(
        noise_seeds,
        obs_count,
        diffusivity,
        wet_mask,
        vert_factor,
        norm_scale,
        obs_cell,
        obs_frac,
    )


def solution(mesh):
    in_specs = (
        P("member"),
        P("tile", None),
        P("tile", None),
        P(),
        P("tile", None),
        P("tile", None, None),
        P("tile", None, None, None),
        P("tile", None),
    )
    out_specs = (P("member", "tile", None), P("tile", None, "member", None))
    return jax.shard_map(body, mesh=mesh, in_specs=in_specs, out_specs=out_specs, check_vma=False)
```

```python
import functools

import jax
import jax.numpy as jnp
from jax import lax
from jax.experimental import pallas as pl
from jax.experimental.pallas import tpu as pltpu
from jax.sharding import PartitionSpec as P

STEPS = 8
GROUP = 8
SPREAD = 3.4641016151377544
MESH = pl.DeviceIdType.MESH


def scramble(hashed):
    hashed = (hashed ^ lax.shift_right_logical(hashed, jnp.int32(16))) * jnp.int32(-2048144789)
    hashed = (hashed ^ lax.shift_right_logical(hashed, jnp.int32(13))) * jnp.int32(-1028477387)
    return hashed ^ lax.shift_right_logical(hashed, jnp.int32(16))


def kernel(
    n,
    seeds_hbm,
    count_hbm,
    diff_hbm,
    wet_hbm,
    vert_hbm,
    scale_hbm,
    cell_hbm,
    frac_hbm,
    pert_ref,
    prof_ref,
    seeds_ref,
    count_ref,
    diff_ref,
    wet_ref,
    vert_ref,
    scale_ref,
    cell_ref,
    frac_ref,
    in_sems,
    edge_send,
    above_recv,
    below_recv,
    next_recv,
    probe_send,
    probe_recv,
    noise,
    work,
    face_rows,
    face_cols,
    wet_all,
    scale_all,
    state,
    vert_pad,
    scaled,
    weights,
    shares,
    field,
    field_rows,
    prof_send,
    prof_recv,
    edge_ss,
    edge_rs,
    probe_ss,
    probe_rs,
    prof_ss,
    prof_rs,
):
    pulls = [
        pltpu.make_async_copy(src, dst, in_sems.at[k])
        for k, (src, dst) in enumerate(
            (
                (diff_hbm, diff_ref),
                (wet_hbm, wet_ref),
                (scale_hbm, scale_ref),
                (seeds_hbm, seeds_ref),
                (count_hbm, count_ref),
                (cell_hbm, cell_ref),
                (frac_hbm, frac_ref),
                (vert_hbm, vert_ref),
            )
        )
    ]
    for pull in pulls:
        pull.start()

    me = lax.axis_index("tile")
    rows, cols = diff_ref.shape
    half = cols // 2
    levels = vert_ref.shape[0]
    padded = state.shape[1]
    groups = padded // GROUP
    slots = cell_ref.shape[2]
    total_rows = n * rows
    span = rows + 2 * STEPS + 1
    kept = rows + 1

    barrier = pltpu.get_barrier_semaphore()

    def greet(k, carry):
        peer = lax.rem(me + k, n)
        pl.semaphore_signal(barrier, inc=1, device_id={"tile": peer}, device_id_type=MESH)
        return carry

    lax.fori_loop(1, n, greet, 0)

    for pull in pulls:
        pull.wait()

    kappa = diff_ref[...] * wet_ref[...].astype(jnp.float32)
    pair_shape = (cols, cols)
    lane = lax.broadcasted_iota(jnp.int32, pair_shape, 1)
    lane = jnp.where(lane < half, 2 * lane, 2 * lane - (cols - 1))
    split = jnp.where(lax.broadcasted_iota(jnp.int32, pair_shape, 0) == lane, 1.0, 0.0)
    plain = jnp.concatenate([kappa, scale_ref[...]], 0)
    high = plain.astype(jnp.bfloat16)
    rest = plain - high.astype(jnp.float32)
    middle = rest.astype(jnp.bfloat16)
    low = (rest - middle.astype(jnp.float32)).astype(jnp.bfloat16)
    dot = functools.partial(jnp.dot, preferred_element_type=jnp.float32)
    terms = dot(jnp.concatenate([high, middle, low], 0), split.astype(jnp.bfloat16))
    edge_send[...] = (terms[0 : 2 * rows] + terms[2 * rows : 4 * rows]) + terms[4 * rows :]
    slot_ids = lax.broadcasted_iota(jnp.int32, (1, slots), 1)

    def pack(h, carry):
        anchor = cell_ref[0, pl.ds(h, 1), :]
        frac = frac_ref[0, h]
        row = lax.shift_right_logical(anchor, jnp.int32(cols.bit_length() - 1))
        col = anchor - row * cols
        probe_send[h, 0:1, :] = col.astype(jnp.float32)
        probe_send[h, 1:2, :] = frac[1:2, :]
        probe_send[h, 2:3, :] = row.astype(jnp.float32)
        probe_send[h, 3:4, :] = frac[0:1, :]
        probe_send[h, 4:8, :] = jnp.zeros((4, slots), jnp.float32)
        return carry

    lax.fori_loop(0, n, pack, 0)

    seed_a = seeds_ref[0]
    seed_b = seeds_ref[1]
    shape = (GROUP, cols)
    col_ids = lax.broadcasted_iota(jnp.int32, shape, 1)
    col_ids = jnp.where(col_ids < half, 2 * col_ids, 2 * col_ids - (cols - 1))
    spread_ids = (
        lax.broadcasted_iota(jnp.int32, shape, 0) * (total_rows * cols) + col_ids
    ) * jnp.int32(-1640531535)
    first_row = me * rows - STEPS

    def draw(g, carry):
        at = pl.multiple_of(g * GROUP, GROUP)
        for j in range(span):
            base = (g * (GROUP * total_rows) + first_row + j) * cols
            hashed = scramble(spread_ids + (base * jnp.int32(-1640531535) + seed_a))
            hashed = scramble(hashed ^ seed_b)
            drawn = lax.shift_right_logical(hashed, jnp.int32(8)).astype(jnp.float32)
            noise[j, pl.ds(at, GROUP), :] = drawn * (SPREAD / 16777216.0) + SPREAD * (
                0.5 / 16777216.0 - 0.5
            )
        return carry

    lax.fori_loop(0, groups // 2, draw, 0)

    pl.semaphore_wait(barrier, n - 1)

    def edge_copy(which):
        if which == 0:
            src, dst, by = edge_send.at[pl.ds(0, rows)], above_recv, 1
        elif which == 1:
            src, dst, by = edge_send, below_recv, n - 1
        else:
            src, dst, by = edge_send.at[pl.ds(0, rows)], next_recv, n - 2
        return pltpu.make_async_remote_copy(
            src_ref=src,
            dst_ref=dst,
            send_sem=edge_ss.at[which],
            recv_sem=edge_rs.at[which],
            device_id={"tile": lax.rem(me + by, n)},
            device_id_type=MESH,
        )

    def probe_copy(peer, slot):
        return pltpu.make_async_remote_copy(
            src_ref=probe_send.at[peer],
            dst_ref=probe_recv.at[slot],
            send_sem=probe_ss.at[peer],
            recv_sem=probe_rs.at[slot],
            device_id={"tile": peer},
            device_id_type=MESH,
        )

    for which in range(3):
        edge_copy(which).start()

    def send_probe(k, carry):
        probe_copy(lax.rem(me + k, n), me).start()
        return carry

    lax.fori_loop(1, n, send_probe, 0)
    probe_recv[me] = probe_send[me]

    lax.fori_loop(groups // 2, groups, draw, 0)

    vert_pad[...] = jnp.zeros_like(vert_pad)
    vert_pad[0:levels, 0:levels] = vert_ref[...]
    vert = vert_pad[:, 0:padded]
    vert_hi = vert.astype(jnp.bfloat16)
    vert_lo = (vert - vert_hi.astype(jnp.float32)).astype(jnp.bfloat16)

    for which in range(3):
        edge_copy(which).wait_recv()

    zero = jnp.zeros((rows, cols), jnp.float32)
    kappa_all = jnp.concatenate(
        [
            jnp.where(me > 0, above_recv[...], zero),
            edge_send[0:rows, :],
            jnp.where(me < n - 1, below_recv[0:rows, :], zero),
            jnp.where(me < n - 2, next_recv[...], zero),
        ],
        0,
    )
    wet = jnp.where(kappa_all > 0.0, 1.0, 0.0)
    even, odd = kappa_all[:, 0:half], kappa_all[:, half:cols]
    last = lax.broadcasted_iota(jnp.int32, even.shape, 1) == half - 1
    faces_in = jnp.sqrt(even * odd)
    faces_out = jnp.where(last, 0.0, jnp.sqrt(odd * pltpu.roll(even, half - 1, 1)))
    faces_c = jnp.concatenate([faces_in, faces_out], 1)
    faces_r = jnp.sqrt(kappa_all[0 : span - 1] * kappa_all[1:span])
    for j in range(span):
        wet_all[j] = jnp.broadcast_to(wet[j : j + 1], shape)
        face_cols[j] = jnp.broadcast_to(faces_c[j : j + 1], shape)
        if j < span - 1:
            face_rows[j] = jnp.broadcast_to(faces_r[j : j + 1], shape)
    for r in range(kept):
        row = edge_send[rows + r : rows + r + 1] if r < rows else below_recv[rows : rows + 1]
        scale_all[r] = jnp.broadcast_to(row, shape)

    def await_probe(k, carry):
        source = lax.rem(me + k, n)
        probe_copy(source, source).wait_recv()
        return carry

    lax.fori_loop(1, n, await_probe, 0)

    pairs = n // 2
    cell_ids = lax.broadcasted_iota(jnp.int32, (cols, 2 * slots), 0)
    cell_ids = jnp.where(cell_ids < half, 2 * cell_ids, 2 * cell_ids - (cols - 1))
    cell_ids = cell_ids.astype(jnp.float32)

    def weigh(pair, carry):
        probes = jnp.concatenate([probe_recv[2 * pair], probe_recv[2 * pair + 1]], 1)
        col, frac_x, row, frac_y = probes[0:1], probes[1:2], probes[2:3], probes[3:4]
        weights[pair] = jnp.where(
            cell_ids == col, 1.0 - frac_x, jnp.where(cell_ids == col + 1.0, frac_x, 0.0)
        ).astype(jnp.bfloat16)
        for r in range(kept):
            shares[pair, r : r + 1, :] = jnp.where(
                row == float(r), 1.0 - frac_y, jnp.where(row == float(r - 1), frac_y, 0.0)
            )
        return carry

    lax.fori_loop(0, pairs, weigh, 0)

    def advance(at):
        def take(ref, j, lo):
            return ref[j, :, lo : lo + half]

        for j in range(span):
            work[j] = noise[j, pl.ds(at, GROUP), :] * wet_all[j]
        for step in range(STEPS):
            here_e, here_o = take(work, step, 0), take(work, step, half)
            up_e = up_o = None
            for j in range(step, span - 1 - step):
                next_e, next_o = take(work, j + 1, 0), take(work, j + 1, half)
                down_e = take(face_rows, j, 0) * (next_e - here_e)
                down_o = take(face_rows, j, half) * (next_o - here_o)
                if j > step:
                    inner = take(face_cols, j, 0) * (here_o - here_e)
                    outer = take(face_cols, j, half) * (
                        pltpu.roll(here_e, half - 1, 1) - here_o
                    )
                    work[j, :, 0:half] = here_e + (
                        (down_e - up_e) + (inner - pltpu.roll(outer, 1, 1))
                    )
                    work[j, :, half:cols] = here_o + ((down_o - up_o) + (outer - inner))
                up_e, up_o = down_e, down_o
                here_e, here_o = next_e, next_o

    def prof_copy(peer, slot, at, size):
        return pltpu.make_async_remote_copy(
            src_ref=prof_send.at[peer, pl.ds(at, size)],
            dst_ref=prof_recv.at[slot, pl.ds(at, size)],
            send_sem=prof_ss.at[peer],
            recv_sem=prof_rs.at[slot],
            device_id={"tile": peer},
            device_id_type=MESH,
        )

    block = 2 * GROUP
    my_pair = me // 2

    def turn(b, carry):
        first = pl.multiple_of(b * block, block)

        def grow(part, inner):
            at = pl.multiple_of(first + part * GROUP, GROUP)
            line = pl.multiple_of(part * GROUP, GROUP)
            advance(at)
            for r in range(kept):
                value = work[STEPS + r]
                if r < rows:
                    state[r, pl.ds(at, GROUP), :] = value
                scaled[r, pl.ds(line, GROUP), :] = value * scale_all[r]
            return inner

        lax.fori_loop(0, 2, grow, 0)
        left = scaled[...].reshape(kept * block, cols).astype(jnp.bfloat16)

        def answer(pair):
            across = jnp.dot(left, weights[pair], preferred_element_type=jnp.float32)
            total = None
            for r in range(kept):
                term = across[r * block : (r + 1) * block] * shares[pair, r : r + 1, :]
                total = term if total is None else total + term
            total = total.astype(jnp.bfloat16)
            prof_send[2 * pair, pl.ds(first, block), :] = total[:, 0:slots]
            prof_send[2 * pair + 1, pl.ds(first, block), :] = total[:, slots : 2 * slots]

        for k in range(1, pairs + 1):
            answer(lax.rem(my_pair + k, pairs))

        def send(k, inner):
            prof_copy(lax.rem(2 * my_pair + 2 + k, n), me, first, block).start()
            return inner

        lax.fori_loop(0, n - 2, send, 0)
        prof_copy(4 * my_pair + 1 - me, me, first, block).start()
        return carry

    lax.fori_loop(0, padded // block, turn, 0)
    prof_recv[me] = prof_send[me]

    for r in range(rows):
        value = state[r]
        high = value.astype(jnp.bfloat16)
        low = (value - high.astype(jnp.float32)).astype(jnp.bfloat16)
        mixed = dot(vert_hi, high) + (dot(vert_hi, low) + dot(vert_lo, high))
        scale = edge_send[rows + r : rows + r + 1, :]
        field[r * padded : (r + 1) * padded, :] = (mixed * scale).astype(jnp.bfloat16)
    lane = lax.broadcasted_iota(jnp.int32, pair_shape, 0)
    lane = jnp.where(lane < half, 2 * lane, 2 * lane - (cols - 1))
    merge = jnp.where(lax.broadcasted_iota(jnp.int32, pair_shape, 1) == lane, 1.0, 0.0)
    merge = merge.astype(jnp.bfloat16)
    for r in range(rows):
        field_rows[:, r, :] = dot(field[r * padded : (r + 1) * padded, :], merge)
    pert_ref[...] = field_rows[0:levels].astype(jnp.bfloat16)

    def await_prof(k, carry):
        source = lax.rem(me + n - k, n)
        prof_copy(source, source, 0, padded).wait_recv()
        return carry

    lax.fori_loop(1, n, await_prof, 0)

    both = jnp.concatenate([vert_hi, vert_lo], 0)
    for source in range(0, n, 2):
        arrived = jnp.concatenate([prof_recv[source], prof_recv[source + 1]], 1)
        mixed = dot(both, arrived)
        mixed = mixed[0:padded] + mixed[padded : 2 * padded]
        for side in range(2):
            live = slot_ids < count_ref[0, source + side]
            mine = mixed[0:levels, side * slots : (side + 1) * slots]
            prof_ref[0, source + side] = jnp.where(live, mine, 0.0).astype(jnp.bfloat16)

    def settle(k, carry):
        peer = lax.rem(me + k, n)
        probe_copy(peer, me).wait_send()
        prof_copy(peer, me, 0, padded).wait_send()
        return carry

    lax.fori_loop(1, n, settle, 0)
    for which in range(3):
        edge_copy(which).wait_send()


def body(
    noise_seeds, diffusivity, wet_mask, vert_factor, norm_scale, obs_cell, obs_frac, obs_count
):
    rows, cols = diffusivity.shape
    levels = vert_factor.shape[0]
    n = lax.axis_size("tile")
    slots = obs_cell.shape[2]
    if rows != STEPS or n % 2 or cols & (cols - 1):
        raise ValueError("unsupported sizes")
    padded = -(-levels // 16) * 16
    span = rows + 2 * STEPS + 1
    kept = rows + 1
    f32, bf16 = jnp.float32, jnp.bfloat16
    vmem = pl.BlockSpec(memory_space=pltpu.VMEM)
    hbm = pl.BlockSpec(memory_space=pltpu.HBM)
    dma = pltpu.SemaphoreType.DMA
    return pl.pallas_call(
        functools.partial(kernel, n),
        out_shape=(
            jax.ShapeDtypeStruct((levels, rows, cols), bf16),
            jax.ShapeDtypeStruct((1, n, levels, slots), bf16),
        ),
        in_specs=[hbm] * 8,
        out_specs=(vmem, vmem),
        scratch_shapes=[
            pltpu.SMEM(noise_seeds.shape, jnp.int32),
            pltpu.SMEM(obs_count.shape, jnp.int32),
            pltpu.VMEM(diffusivity.shape, f32),
            pltpu.VMEM(wet_mask.shape, jnp.int32),
            pltpu.VMEM(vert_factor.shape, f32),
            pltpu.VMEM(norm_scale.shape, f32),
            pltpu.VMEM(obs_cell.shape, jnp.int32),
            pltpu.VMEM(obs_frac.shape, f32),
            dma((8,)),
            pltpu.VMEM((2 * rows, cols), f32),
            pltpu.VMEM((rows, cols), f32),
            pltpu.VMEM((2 * rows, cols), f32),
            pltpu.VMEM((rows, cols), f32),
            pltpu.VMEM((n, 8, slots), f32),
            pltpu.VMEM((n, 8, slots), f32),
            pltpu.VMEM((span, padded, cols), f32),
            pltpu.VMEM((span, GROUP, cols), f32),
            pltpu.VMEM((span, GROUP, cols), f32),
            pltpu.VMEM((span, GROUP, cols), f32),
            pltpu.VMEM((span, GROUP, cols), f32),
            pltpu.VMEM((kept, GROUP, cols), f32),
            pltpu.VMEM((rows, padded, cols), f32),
            pltpu.VMEM((padded, 128), f32),
            pltpu.VMEM((kept, 2 * GROUP, cols), f32),
            pltpu.VMEM((n // 2, cols, 2 * slots), bf16),
            pltpu.VMEM((n // 2, 2 * GROUP, 2 * slots), f32),
            pltpu.VMEM((rows * padded, cols), bf16),
            pltpu.VMEM((padded, rows, cols), f32),
            pltpu.VMEM((n, padded, slots), bf16),
            pltpu.VMEM((n, padded, slots), bf16),
            dma((3,)),
            dma((3,)),
            dma((n,)),
            dma((n,)),
            dma((n,)),
            dma((n,)),
        ],
        compiler_params=pltpu.CompilerParams(
            collective_id=0, has_side_effects=True, vmem_limit_bytes=60 * 1024 * 1024
        ),
    )(
        noise_seeds,
        obs_count,
        diffusivity,
        wet_mask,
        vert_factor,
        norm_scale,
        obs_cell,
        obs_frac,
    )


def solution(mesh):
    in_specs = (
        P("member"),
        P("tile", None),
        P("tile", None),
        P(),
        P("tile", None),
        P("tile", None, None),
        P("tile", None, None, None),
        P("tile", None),
    )
    out_specs = (P("member", "tile", None), P("tile", None, "member", None))
    return jax.shard_map(body, mesh=mesh, in_specs=in_specs, out_specs=out_specs, check_vma=False)
```

```python
import functools

import jax
import jax.numpy as jnp
from jax import lax
from jax.experimental import pallas as pl
from jax.experimental.pallas import tpu as pltpu
from jax.sharding import PartitionSpec as P

STEPS = 8
GROUP = 8
SPREAD = 3.4641016151377544
MESH = pl.DeviceIdType.MESH


def scramble(hashed):
    hashed = (hashed ^ lax.shift_right_logical(hashed, jnp.int32(16))) * jnp.int32(-2048144789)
    hashed = (hashed ^ lax.shift_right_logical(hashed, jnp.int32(13))) * jnp.int32(-1028477387)
    return hashed ^ lax.shift_right_logical(hashed, jnp.int32(16))


def kernel(
    n,
    seeds_hbm,
    count_hbm,
    diff_hbm,
    wet_hbm,
    vert_hbm,
    scale_hbm,
    cell_hbm,
    frac_hbm,
    pert_ref,
    prof_ref,
    seeds_ref,
    count_ref,
    diff_ref,
    wet_ref,
    vert_ref,
    scale_ref,
    cell_ref,
    frac_ref,
    in_sems,
    edge_send,
    above_recv,
    below_recv,
    next_recv,
    probe_send,
    probe_recv,
    noise,
    work,
    face_rows,
    face_cols,
    face_left,
    wet_all,
    scale_all,
    state,
    vert_pad,
    scaled,
    weights,
    shares,
    field,
    field_rows,
    prof_send,
    prof_recv,
    edge_ss,
    edge_rs,
    probe_ss,
    probe_rs,
    prof_ss,
    prof_rs,
):
    pulls = [
        pltpu.make_async_copy(src, dst, in_sems.at[k])
        for k, (src, dst) in enumerate(
            (
                (diff_hbm, diff_ref),
                (wet_hbm, wet_ref),
                (scale_hbm, scale_ref),
                (seeds_hbm, seeds_ref),
                (count_hbm, count_ref),
                (cell_hbm, cell_ref),
                (frac_hbm, frac_ref),
                (vert_hbm, vert_ref),
            )
        )
    ]
    for pull in pulls:
        pull.start()

    me = lax.axis_index("tile")
    rows, cols = diff_ref.shape
    half = cols // 2
    levels = vert_ref.shape[0]
    padded = state.shape[1]
    groups = padded // GROUP
    slots = cell_ref.shape[2]
    total_rows = n * rows
    span = rows + 2 * STEPS + 1
    kept = rows + 1

    barrier = pltpu.get_barrier_semaphore()

    def greet(k, carry):
        peer = lax.rem(me + k, n)
        pl.semaphore_signal(barrier, inc=1, device_id={"tile": peer}, device_id_type=MESH)
        return carry

    lax.fori_loop(1, n, greet, 0)

    for pull in pulls:
        pull.wait()

    kappa = diff_ref[...] * wet_ref[...].astype(jnp.float32)
    pair_shape = (cols, cols)
    lane = lax.broadcasted_iota(jnp.int32, pair_shape, 1)
    lane = jnp.where(lane < half, 2 * lane, 2 * lane - (cols - 1))
    split = jnp.where(lax.broadcasted_iota(jnp.int32, pair_shape, 0) == lane, 1.0, 0.0)
    plain = jnp.concatenate([kappa, scale_ref[...]], 0)
    high = plain.astype(jnp.bfloat16)
    rest = plain - high.astype(jnp.float32)
    middle = rest.astype(jnp.bfloat16)
    low = (rest - middle.astype(jnp.float32)).astype(jnp.bfloat16)
    dot = functools.partial(jnp.dot, preferred_element_type=jnp.float32)
    terms = dot(jnp.concatenate([high, middle, low], 0), split.astype(jnp.bfloat16))
    edge_send[...] = (terms[0 : 2 * rows] + terms[2 * rows : 4 * rows]) + terms[4 * rows :]
    slot_ids = lax.broadcasted_iota(jnp.int32, (1, slots), 1)

    def pack(h, carry):
        anchor = cell_ref[0, pl.ds(h, 1), :]
        frac = frac_ref[0, h]
        row = lax.shift_right_logical(anchor, jnp.int32(cols.bit_length() - 1))
        col = anchor - row * cols
        probe_send[h, 0:1, :] = col.astype(jnp.float32)
        probe_send[h, 1:2, :] = frac[1:2, :]
        probe_send[h, 2:3, :] = row.astype(jnp.float32)
        probe_send[h, 3:4, :] = frac[0:1, :]
        probe_send[h, 4:8, :] = jnp.zeros((4, slots), jnp.float32)
        return carry

    lax.fori_loop(0, n, pack, 0)

    seed_a = seeds_ref[0]
    seed_b = seeds_ref[1]
    shape = (GROUP, cols)
    col_ids = lax.broadcasted_iota(jnp.int32, shape, 1)
    col_ids = jnp.where(col_ids < half, 2 * col_ids, 2 * col_ids - (cols - 1))
    spread_ids = (
        lax.broadcasted_iota(jnp.int32, shape, 0) * (total_rows * cols) + col_ids
    ) * jnp.int32(-1640531535)
    first_row = me * rows - STEPS

    def draw(g, carry):
        at = pl.multiple_of(g * GROUP, GROUP)
        for j in range(span):
            base = (g * (GROUP * total_rows) + first_row + j) * cols
            hashed = scramble(spread_ids + (base * jnp.int32(-1640531535) + seed_a))
            hashed = scramble(hashed ^ seed_b)
            drawn = lax.shift_right_logical(hashed, jnp.int32(8)).astype(jnp.float32)
            noise[j, pl.ds(at, GROUP), :] = drawn * (SPREAD / 16777216.0) + SPREAD * (
                0.5 / 16777216.0 - 0.5
            )
        return carry

    lax.fori_loop(0, groups // 2, draw, 0)

    pl.semaphore_wait(barrier, n - 1)

    def edge_copy(which):
        if which == 0:
            src, dst, by = edge_send.at[pl.ds(0, rows)], above_recv, 1
        elif which == 1:
            src, dst, by = edge_send, below_recv, n - 1
        else:
            src, dst, by = edge_send.at[pl.ds(0, rows)], next_recv, n - 2
        return pltpu.make_async_remote_copy(
            src_ref=src,
            dst_ref=dst,
            send_sem=edge_ss.at[which],
            recv_sem=edge_rs.at[which],
            device_id={"tile": lax.rem(me + by, n)},
            device_id_type=MESH,
        )

    def probe_copy(peer, slot):
        return pltpu.make_async_remote_copy(
            src_ref=probe_send.at[peer],
            dst_ref=probe_recv.at[slot],
            send_sem=probe_ss.at[peer],
            recv_sem=probe_rs.at[slot],
            device_id={"tile": peer},
            device_id_type=MESH,
        )

    for which in range(3):
        edge_copy(which).start()

    def send_probe(k, carry):
        probe_copy(lax.rem(me + k, n), me).start()
        return carry

    lax.fori_loop(1, n, send_probe, 0)
    probe_recv[me] = probe_send[me]

    lax.fori_loop(groups // 2, groups, draw, 0)

    vert_pad[...] = jnp.zeros_like(vert_pad)
    vert_pad[0:levels, 0:levels] = vert_ref[...]
    vert = vert_pad[:, 0:padded]
    vert_hi = vert.astype(jnp.bfloat16)
    vert_lo = (vert - vert_hi.astype(jnp.float32)).astype(jnp.bfloat16)

    for which in range(3):
        edge_copy(which).wait_recv()

    zero = jnp.zeros((rows, cols), jnp.float32)
    kappa_all = jnp.concatenate(
        [
            jnp.where(me > 0, above_recv[...], zero),
            edge_send[0:rows, :],
            jnp.where(me < n - 1, below_recv[0:rows, :], zero),
            jnp.where(me < n - 2, next_recv[...], zero),
        ],
        0,
    )
    wet = jnp.where(kappa_all > 0.0, 1.0, 0.0)
    even, odd = kappa_all[:, 0:half], kappa_all[:, half:cols]
    last = lax.broadcasted_iota(jnp.int32, even.shape, 1) == half - 1
    faces_in = jnp.sqrt(even * odd)
    faces_out = jnp.where(last, 0.0, jnp.sqrt(odd * pltpu.roll(even, half - 1, 1)))
    faces_c = jnp.concatenate([faces_in, faces_out], 1)
    faces_left = pltpu.roll(faces_out, 1, 1)
    faces_r = jnp.sqrt(kappa_all[0 : span - 1] * kappa_all[1:span])
    for j in range(span):
        wet_all[j] = jnp.broadcast_to(wet[j : j + 1], shape)
        face_cols[j] = jnp.broadcast_to(faces_c[j : j + 1], shape)
        face_left[j] = jnp.broadcast_to(faces_left[j : j + 1], (GROUP, half))
        if j < span - 1:
            face_rows[j] = jnp.broadcast_to(faces_r[j : j + 1], shape)
    for r in range(kept):
        row = edge_send[rows + r : rows + r + 1] if r < rows else below_recv[rows : rows + 1]
        scale_all[r] = jnp.broadcast_to(row, shape)

    def await_probe(k, carry):
        source = lax.rem(me + k, n)
        probe_copy(source, source).wait_recv()
        return carry

    lax.fori_loop(1, n, await_probe, 0)

    pairs = n // 2
    cell_ids = lax.broadcasted_iota(jnp.int32, (cols, 2 * slots), 0)
    cell_ids = jnp.where(cell_ids < half, 2 * cell_ids, 2 * cell_ids - (cols - 1))
    cell_ids = cell_ids.astype(jnp.float32)

    def weigh(pair, carry):
        probes = jnp.concatenate([probe_recv[2 * pair], probe_recv[2 * pair + 1]], 1)
        col, frac_x, row, frac_y = probes[0:1], probes[1:2], probes[2:3], probes[3:4]
        weights[pair] = jnp.where(
            cell_ids == col, 1.0 - frac_x, jnp.where(cell_ids == col + 1.0, frac_x, 0.0)
        ).astype(jnp.bfloat16)
        for r in range(kept):
            shares[pair, r : r + 1, :] = jnp.where(
                row == float(r), 1.0 - frac_y, jnp.where(row == float(r - 1), frac_y, 0.0)
            )
        return carry

    lax.fori_loop(0, pairs, weigh, 0)

    def advance(first):
        def take(ref, j, lo):
            return ref[j, :, lo : lo + half]

        parts = [pl.ds(part * GROUP, GROUP) for part in range(2)]
        for j in range(span):
            for part in range(2):
                at = pl.multiple_of(first + part * GROUP, GROUP)
                work[j, parts[part], :] = noise[j, pl.ds(at, GROUP), :] * wet_all[j]
        for step in range(STEPS):
            here = [
                (work[step, part, 0:half], work[step, part, half:cols]) for part in parts
            ]
            up = [None, None]
            for j in range(step, span - 1 - step):
                rows_e, rows_o = take(face_rows, j, 0), take(face_rows, j, half)
                if j > step:
                    cols_in = take(face_cols, j, 0)
                    cols_right = take(face_cols, j, half)
                    cols_left = face_left[j]
                for k, part in enumerate(parts):
                    here_e, here_o = here[k]
                    next_e, next_o = work[j + 1, part, 0:half], work[j + 1, part, half:cols]
                    down_e = rows_e * (next_e - here_e)
                    down_o = rows_o * (next_o - here_o)
                    if j > step:
                        up_e, up_o = up[k]
                        inner = cols_in * (here_o - here_e)
                        right = cols_right * (pltpu.roll(here_e, half - 1, 1) - here_o)
                        left = cols_left * (here_e - pltpu.roll(here_o, 1, 1))
                        work[j, part, 0:half] = here_e + ((down_e - up_e) + (inner - left))
                        work[j, part, half:cols] = here_o + ((down_o - up_o) + (right - inner))
                    up[k] = (down_e, down_o)
                    here[k] = (next_e, next_o)

    def prof_copy(peer, slot, at, size):
        return pltpu.make_async_remote_copy(
            src_ref=prof_send.at[peer, pl.ds(at, size)],
            dst_ref=prof_recv.at[slot, pl.ds(at, size)],
            send_sem=prof_ss.at[peer],
            recv_sem=prof_rs.at[slot],
            device_id={"tile": peer},
            device_id_type=MESH,
        )

    block = 2 * GROUP
    my_pair = me // 2

    def turn(b, carry):
        first = pl.multiple_of(b * block, block)

        advance(first)
        for r in range(kept):
            for part in range(2):
                here = pl.ds(part * GROUP, GROUP)
                value = work[STEPS + r, here, :]
                if r < rows:
                    at = pl.multiple_of(first + part * GROUP, GROUP)
                    state[r, pl.ds(at, GROUP), :] = value
                scaled[r, here, :] = value * scale_all[r]
        left = scaled[...].reshape(kept * block, cols).astype(jnp.bfloat16)

        def answer(pair):
            across = jnp.dot(left, weights[pair], preferred_element_type=jnp.float32)
            total = None
            for r in range(kept):
                term = across[r * block : (r + 1) * block] * shares[pair, r : r + 1, :]
                total = term if total is None else total + term
            total = total.astype(jnp.bfloat16)
            prof_send[2 * pair, pl.ds(first, block), :] = total[:, 0:slots]
            prof_send[2 * pair + 1, pl.ds(first, block), :] = total[:, slots : 2 * slots]

        for k in range(1, pairs + 1):
            answer(lax.rem(my_pair + k, pairs))

        def send(k, inner):
            prof_copy(lax.rem(2 * my_pair + 2 + k, n), me, first, block).start()
            return inner

        lax.fori_loop(0, n - 2, send, 0)
        prof_copy(4 * my_pair + 1 - me, me, first, block).start()
        return carry

    lax.fori_loop(0, padded // block, turn, 0)
    prof_recv[me] = prof_send[me]

    for r in range(rows):
        value = state[r]
        high = value.astype(jnp.bfloat16)
        low = (value - high.astype(jnp.float32)).astype(jnp.bfloat16)
        mixed = dot(vert_hi, high) + (dot(vert_hi, low) + dot(vert_lo, high))
        scale = edge_send[rows + r : rows + r + 1, :]
        field[r * padded : (r + 1) * padded, :] = (mixed * scale).astype(jnp.bfloat16)
    lane = lax.broadcasted_iota(jnp.int32, pair_shape, 0)
    lane = jnp.where(lane < half, 2 * lane, 2 * lane - (cols - 1))
    merge = jnp.where(lax.broadcasted_iota(jnp.int32, pair_shape, 1) == lane, 1.0, 0.0)
    merge = merge.astype(jnp.bfloat16)
    for r in range(rows):
        field_rows[:, r, :] = dot(field[r * padded : (r + 1) * padded, :], merge)
    pert_ref[...] = field_rows[0:levels].astype(jnp.bfloat16)

    def await_prof(k, carry):
        source = lax.rem(me + n - k, n)
        prof_copy(source, source, 0, padded).wait_recv()
        return carry

    lax.fori_loop(1, n, await_prof, 0)

    both = jnp.concatenate([vert_hi, vert_lo], 0)
    for source in range(0, n, 2):
        arrived = jnp.concatenate([prof_recv[source], prof_recv[source + 1]], 1)
        mixed = dot(both, arrived)
        mixed = mixed[0:padded] + mixed[padded : 2 * padded]
        for side in range(2):
            live = slot_ids < count_ref[0, source + side]
            mine = mixed[0:levels, side * slots : (side + 1) * slots]
            prof_ref[0, source + side] = jnp.where(live, mine, 0.0).astype(jnp.bfloat16)

    def settle(k, carry):
        peer = lax.rem(me + k, n)
        probe_copy(peer, me).wait_send()
        prof_copy(peer, me, 0, padded).wait_send()
        return carry

    lax.fori_loop(1, n, settle, 0)
    for which in range(3):
        edge_copy(which).wait_send()


def body(
    noise_seeds, diffusivity, wet_mask, vert_factor, norm_scale, obs_cell, obs_frac, obs_count
):
    rows, cols = diffusivity.shape
    levels = vert_factor.shape[0]
    n = lax.axis_size("tile")
    slots = obs_cell.shape[2]
    if rows != STEPS or n % 2 or cols & (cols - 1):
        raise ValueError("unsupported sizes")
    padded = -(-levels // 16) * 16
    span = rows + 2 * STEPS + 1
    kept = rows + 1
    f32, bf16 = jnp.float32, jnp.bfloat16
    vmem = pl.BlockSpec(memory_space=pltpu.VMEM)
    hbm = pl.BlockSpec(memory_space=pltpu.HBM)
    dma = pltpu.SemaphoreType.DMA
    return pl.pallas_call(
        functools.partial(kernel, n),
        out_shape=(
            jax.ShapeDtypeStruct((levels, rows, cols), bf16),
            jax.ShapeDtypeStruct((1, n, levels, slots), bf16),
        ),
        in_specs=[hbm] * 8,
        out_specs=(vmem, vmem),
        scratch_shapes=[
            pltpu.SMEM(noise_seeds.shape, jnp.int32),
            pltpu.SMEM(obs_count.shape, jnp.int32),
            pltpu.VMEM(diffusivity.shape, f32),
            pltpu.VMEM(wet_mask.shape, jnp.int32),
            pltpu.VMEM(vert_factor.shape, f32),
            pltpu.VMEM(norm_scale.shape, f32),
            pltpu.VMEM(obs_cell.shape, jnp.int32),
            pltpu.VMEM(obs_frac.shape, f32),
            dma((8,)),
            pltpu.VMEM((2 * rows, cols), f32),
            pltpu.VMEM((rows, cols), f32),
            pltpu.VMEM((2 * rows, cols), f32),
            pltpu.VMEM((rows, cols), f32),
            pltpu.VMEM((n, 8, slots), f32),
            pltpu.VMEM((n, 8, slots), f32),
            pltpu.VMEM((span, padded, cols), f32),
            pltpu.VMEM((span, 2 * GROUP, cols), f32),
            pltpu.VMEM((span, GROUP, cols), f32),
            pltpu.VMEM((span, GROUP, cols), f32),
            pltpu.VMEM((span, GROUP, cols // 2), f32),
            pltpu.VMEM((span, GROUP, cols), f32),
            pltpu.VMEM((kept, GROUP, cols), f32),
            pltpu.VMEM((rows, padded, cols), f32),
            pltpu.VMEM((padded, 128), f32),
            pltpu.VMEM((kept, 2 * GROUP, cols), f32),
            pltpu.VMEM((n // 2, cols, 2 * slots), bf16),
            pltpu.VMEM((n // 2, 2 * GROUP, 2 * slots), f32),
            pltpu.VMEM((rows * padded, cols), bf16),
            pltpu.VMEM((padded, rows, cols), f32),
            pltpu.VMEM((n, padded, slots), bf16),
            pltpu.VMEM((n, padded, slots), bf16),
            dma((3,)),
            dma((3,)),
            dma((n,)),
            dma((n,)),
            dma((n,)),
            dma((n,)),
        ],
        compiler_params=pltpu.CompilerParams(
            collective_id=0, has_side_effects=True, vmem_limit_bytes=60 * 1024 * 1024
        ),
    )(
        noise_seeds,
        obs_count,
        diffusivity,
        wet_mask,
        vert_factor,
        norm_scale,
        obs_cell,
        obs_frac,
    )


def solution(mesh):
    in_specs = (
        P("member"),
        P("tile", None),
        P("tile", None),
        P(),
        P("tile", None),
        P("tile", None, None),
        P("tile", None, None, None),
        P("tile", None),
    )
    out_specs = (P("member", "tile", None), P("tile", None, "member", None))
    return jax.shard_map(body, mesh=mesh, in_specs=in_specs, out_specs=out_specs, check_vma=False)
```

```python
import functools

import jax
import jax.numpy as jnp
from jax import lax
from jax.experimental import pallas as pl
from jax.experimental.pallas import tpu as pltpu
from jax.sharding import PartitionSpec as P

STEPS = 8
GROUP = 8
SPREAD = 3.4641016151377544
MESH = pl.DeviceIdType.MESH


def scramble(hashed):
    hashed = (hashed ^ lax.shift_right_logical(hashed, jnp.int32(16))) * jnp.int32(-2048144789)
    hashed = (hashed ^ lax.shift_right_logical(hashed, jnp.int32(13))) * jnp.int32(-1028477387)
    return hashed ^ lax.shift_right_logical(hashed, jnp.int32(16))


def kernel(
    n,
    seeds_hbm,
    count_hbm,
    diff_hbm,
    wet_hbm,
    vert_hbm,
    scale_hbm,
    cell_hbm,
    frac_hbm,
    pert_ref,
    prof_ref,
    seeds_ref,
    count_ref,
    diff_ref,
    wet_ref,
    vert_ref,
    scale_ref,
    cell_ref,
    frac_ref,
    in_sems,
    edge_send,
    above_recv,
    below_recv,
    next_recv,
    probe_send,
    probe_recv,
    noise,
    work,
    face_rows,
    face_cols,
    face_left,
    wet_all,
    scale_all,
    state,
    vert_pad,
    scaled,
    weights,
    shares,
    field,
    field_rows,
    prof_send,
    prof_recv,
    edge_ss,
    edge_rs,
    probe_ss,
    probe_rs,
    prof_ss,
    prof_rs,
):
    pulls = [
        pltpu.make_async_copy(src, dst, in_sems.at[k])
        for k, (src, dst) in enumerate(
            (
                (seeds_hbm, seeds_ref),
                (diff_hbm, diff_ref),
                (wet_hbm, wet_ref),
                (scale_hbm, scale_ref),
                (count_hbm, count_ref),
                (cell_hbm, cell_ref),
                (frac_hbm, frac_ref),
                (vert_hbm, vert_ref),
            )
        )
    ]
    for pull in pulls:
        pull.start()

    me = lax.axis_index("tile")
    rows, cols = diff_ref.shape
    half = cols // 2
    levels = vert_ref.shape[0]
    padded = state.shape[1]
    groups = padded // GROUP
    slots = cell_ref.shape[2]
    total_rows = n * rows
    span = rows + 2 * STEPS + 1
    kept = rows + 1

    barrier = pltpu.get_barrier_semaphore()

    def greet(k, carry):
        peer = lax.rem(me + k, n)
        pl.semaphore_signal(barrier, inc=1, device_id={"tile": peer}, device_id_type=MESH)
        return carry

    lax.fori_loop(1, n, greet, 0)

    pulls[0].wait()
    seed_a = seeds_ref[0]
    seed_b = seeds_ref[1]
    shape = (GROUP, cols)
    col_ids = lax.broadcasted_iota(jnp.int32, shape, 1)
    col_ids = jnp.where(col_ids < half, 2 * col_ids, 2 * col_ids - (cols - 1))
    spread_ids = (
        lax.broadcasted_iota(jnp.int32, shape, 0) * (total_rows * cols) + col_ids
    ) * jnp.int32(-1640531535)
    first_row = me * rows - STEPS

    def draw(g, carry):
        at = pl.multiple_of(g * GROUP, GROUP)
        for j in range(span):
            base = (g * (GROUP * total_rows) + first_row + j) * cols
            hashed = scramble(spread_ids + (base * jnp.int32(-1640531535) + seed_a))
            hashed = scramble(hashed ^ seed_b)
            drawn = lax.shift_right_logical(hashed, jnp.int32(8)).astype(jnp.float32)
            noise[j, pl.ds(at, GROUP), :] = drawn * (SPREAD / 16777216.0) + SPREAD * (
                0.5 / 16777216.0 - 0.5
            )
        return carry

    lax.fori_loop(0, groups // 2, draw, 0)

    for pull in pulls[1:]:
        pull.wait()

    kappa = diff_ref[...] * wet_ref[...].astype(jnp.float32)
    pair_shape = (cols, cols)
    lane = lax.broadcasted_iota(jnp.int32, pair_shape, 1)
    lane = jnp.where(lane < half, 2 * lane, 2 * lane - (cols - 1))
    split = jnp.where(lax.broadcasted_iota(jnp.int32, pair_shape, 0) == lane, 1.0, 0.0)
    plain = jnp.concatenate([kappa, scale_ref[...]], 0)
    high = plain.astype(jnp.bfloat16)
    rest = plain - high.astype(jnp.float32)
    middle = rest.astype(jnp.bfloat16)
    low = (rest - middle.astype(jnp.float32)).astype(jnp.bfloat16)
    dot = functools.partial(jnp.dot, preferred_element_type=jnp.float32)
    terms = dot(jnp.concatenate([high, middle, low], 0), split.astype(jnp.bfloat16))
    edge_send[...] = (terms[0 : 2 * rows] + terms[2 * rows : 4 * rows]) + terms[4 * rows :]
    slot_ids = lax.broadcasted_iota(jnp.int32, (1, slots), 1)

    anchor = cell_ref[0]
    row = lax.shift_right_logical(anchor, jnp.int32(cols.bit_length() - 1))
    probe_send[:, 0, :] = (anchor - row * cols).astype(jnp.float32)
    probe_send[:, 1, :] = frac_ref[0, :, 1, :]
    probe_send[:, 2, :] = row.astype(jnp.float32)
    probe_send[:, 3, :] = frac_ref[0, :, 0, :]
    for k in range(4, 8):
        probe_send[:, k, :] = jnp.zeros(anchor.shape, jnp.float32)

    pl.semaphore_wait(barrier, n - 1)

    def edge_copy(which):
        if which == 0:
            src, dst, by = edge_send.at[pl.ds(0, rows)], above_recv, 1
        elif which == 1:
            src, dst, by = edge_send, below_recv, n - 1
        else:
            src, dst, by = edge_send.at[pl.ds(0, rows)], next_recv, n - 2
        return pltpu.make_async_remote_copy(
            src_ref=src,
            dst_ref=dst,
            send_sem=edge_ss.at[which],
            recv_sem=edge_rs.at[which],
            device_id={"tile": lax.rem(me + by, n)},
            device_id_type=MESH,
        )

    def probe_copy(peer, slot):
        return pltpu.make_async_remote_copy(
            src_ref=probe_send.at[peer],
            dst_ref=probe_recv.at[slot],
            send_sem=probe_ss.at[peer],
            recv_sem=probe_rs.at[slot],
            device_id={"tile": peer},
            device_id_type=MESH,
        )

    for which in range(3):
        edge_copy(which).start()

    def send_probe(k, carry):
        probe_copy(lax.rem(me + k, n), me).start()
        return carry

    lax.fori_loop(1, n, send_probe, 0)
    probe_recv[me] = probe_send[me]

    lax.fori_loop(groups // 2, groups, draw, 0)

    vert_pad[...] = jnp.zeros_like(vert_pad)
    vert_pad[0:levels, 0:levels] = vert_ref[...]
    vert = vert_pad[:, 0:padded]
    vert_hi = vert.astype(jnp.bfloat16)
    vert_lo = (vert - vert_hi.astype(jnp.float32)).astype(jnp.bfloat16)

    for which in range(3):
        edge_copy(which).wait_recv()

    zero = jnp.zeros((rows, cols), jnp.float32)
    kappa_all = jnp.concatenate(
        [
            jnp.where(me > 0, above_recv[...], zero),
            edge_send[0:rows, :],
            jnp.where(me < n - 1, below_recv[0:rows, :], zero),
            jnp.where(me < n - 2, next_recv[...], zero),
        ],
        0,
    )
    wet = jnp.where(kappa_all > 0.0, 1.0, 0.0)
    even, odd = kappa_all[:, 0:half], kappa_all[:, half:cols]
    last = lax.broadcasted_iota(jnp.int32, even.shape, 1) == half - 1
    faces_in = jnp.sqrt(even * odd)
    faces_out = jnp.where(last, 0.0, jnp.sqrt(odd * pltpu.roll(even, half - 1, 1)))
    faces_c = jnp.concatenate([faces_in, faces_out], 1)
    faces_left = pltpu.roll(faces_out, 1, 1)
    faces_r = jnp.sqrt(kappa_all[0 : span - 1] * kappa_all[1:span])
    for j in range(span):
        wet_all[j] = jnp.broadcast_to(wet[j : j + 1], shape)
        face_cols[j] = jnp.broadcast_to(faces_c[j : j + 1], shape)
        face_left[j] = jnp.broadcast_to(faces_left[j : j + 1], (GROUP, half))
        if j < span - 1:
            face_rows[j] = jnp.broadcast_to(faces_r[j : j + 1], shape)
    for r in range(kept):
        row = edge_send[rows + r : rows + r + 1] if r < rows else below_recv[rows : rows + 1]
        scale_all[r] = jnp.broadcast_to(row, shape)

    def await_probe(k, carry):
        source = lax.rem(me + k, n)
        probe_copy(source, source).wait_recv()
        return carry

    lax.fori_loop(1, n, await_probe, 0)

    pairs = n // 2
    cell_ids = lax.broadcasted_iota(jnp.int32, (cols, 2 * slots), 0)
    cell_ids = jnp.where(cell_ids < half, 2 * cell_ids, 2 * cell_ids - (cols - 1))
    cell_ids = cell_ids.astype(jnp.float32)

    def weigh(pair, carry):
        probes = jnp.concatenate([probe_recv[2 * pair], probe_recv[2 * pair + 1]], 1)
        col, frac_x, row, frac_y = probes[0:1], probes[1:2], probes[2:3], probes[3:4]
        weights[pair] = jnp.where(
            cell_ids == col, 1.0 - frac_x, jnp.where(cell_ids == col + 1.0, frac_x, 0.0)
        ).astype(jnp.bfloat16)
        for r in range(kept):
            shares[pair, r : r + 1, :] = jnp.where(
                row == float(r), 1.0 - frac_y, jnp.where(row == float(r - 1), frac_y, 0.0)
            )
        return carry

    lax.fori_loop(0, pairs, weigh, 0)

    def advance(first):
        def take(ref, j, lo):
            return ref[j, :, lo : lo + half]

        parts = [pl.ds(part * GROUP, GROUP) for part in range(2)]
        for j in range(span):
            for part in range(2):
                at = pl.multiple_of(first + part * GROUP, GROUP)
                work[j, parts[part], :] = noise[j, pl.ds(at, GROUP), :] * wet_all[j]
        for step in range(STEPS):
            here = [
                (work[step, part, 0:half], work[step, part, half:cols]) for part in parts
            ]
            up = [None, None]
            for j in range(step, span - 1 - step):
                rows_e, rows_o = take(face_rows, j, 0), take(face_rows, j, half)
                if j > step:
                    cols_in = take(face_cols, j, 0)
                    cols_right = take(face_cols, j, half)
                    cols_left = face_left[j]
                for k, part in enumerate(parts):
                    here_e, here_o = here[k]
                    next_e, next_o = work[j + 1, part, 0:half], work[j + 1, part, half:cols]
                    down_e = rows_e * (next_e - here_e)
                    down_o = rows_o * (next_o - here_o)
                    if j > step:
                        up_e, up_o = up[k]
                        inner = cols_in * (here_o - here_e)
                        right = cols_right * (pltpu.roll(here_e, half - 1, 1) - here_o)
                        left = cols_left * (here_e - pltpu.roll(here_o, 1, 1))
                        work[j, part, 0:half] = here_e + ((down_e - up_e) + (inner - left))
                        work[j, part, half:cols] = here_o + ((down_o - up_o) + (right - inner))
                    up[k] = (down_e, down_o)
                    here[k] = (next_e, next_o)

    def prof_copy(peer, slot, at, size):
        return pltpu.make_async_remote_copy(
            src_ref=prof_send.at[peer, pl.ds(at, size)],
            dst_ref=prof_recv.at[slot, pl.ds(at, size)],
            send_sem=prof_ss.at[peer],
            recv_sem=prof_rs.at[slot],
            device_id={"tile": peer},
            device_id_type=MESH,
        )

    block = 2 * GROUP
    my_pair = me // 2

    def turn(b, carry):
        first = pl.multiple_of(b * block, block)

        advance(first)
        for r in range(kept):
            for part in range(2):
                here = pl.ds(part * GROUP, GROUP)
                value = work[STEPS + r, here, :]
                if r < rows:
                    at = pl.multiple_of(first + part * GROUP, GROUP)
                    state[r, pl.ds(at, GROUP), :] = value
                scaled[r, here, :] = value * scale_all[r]
        left = scaled[...].reshape(kept * block, cols).astype(jnp.bfloat16)

        def answer(pair):
            across = jnp.dot(left, weights[pair], preferred_element_type=jnp.float32)
            total = None
            for r in range(kept):
                term = across[r * block : (r + 1) * block] * shares[pair, r : r + 1, :]
                total = term if total is None else total + term
            total = total.astype(jnp.bfloat16)
            prof_send[2 * pair, pl.ds(first, block), :] = total[:, 0:slots]
            prof_send[2 * pair + 1, pl.ds(first, block), :] = total[:, slots : 2 * slots]

        for k in range(1, pairs + 1):
            answer(lax.rem(my_pair + k, pairs))

        for k in range(n - 2):
            prof_copy(lax.rem(2 * my_pair + 2 + k, n), me, first, block).start()
        prof_copy(4 * my_pair + 1 - me, me, first, block).start()
        return carry

    lax.fori_loop(0, padded // block, turn, 0)
    prof_recv[me] = prof_send[me]

    for r in range(rows):
        value = state[r]
        high = value.astype(jnp.bfloat16)
        low = (value - high.astype(jnp.float32)).astype(jnp.bfloat16)
        mixed = dot(vert_hi, high) + (dot(vert_hi, low) + dot(vert_lo, high))
        scale = edge_send[rows + r : rows + r + 1, :]
        field[r * padded : (r + 1) * padded, :] = (mixed * scale).astype(jnp.bfloat16)
    lane = lax.broadcasted_iota(jnp.int32, pair_shape, 0)
    lane = jnp.where(lane < half, 2 * lane, 2 * lane - (cols - 1))
    merge = jnp.where(lax.broadcasted_iota(jnp.int32, pair_shape, 1) == lane, 1.0, 0.0)
    merge = merge.astype(jnp.bfloat16)
    for r in range(rows):
        field_rows[:, r, :] = dot(field[r * padded : (r + 1) * padded, :], merge)
    pert_ref[...] = field_rows[0:levels].astype(jnp.bfloat16)

    def await_prof(k, carry):
        source = lax.rem(me + n - k, n)
        prof_copy(source, source, 0, padded).wait_recv()
        return carry

    lax.fori_loop(1, n, await_prof, 0)

    both = jnp.concatenate([vert_hi, vert_lo], 0)
    for source in range(0, n, 2):
        arrived = jnp.concatenate([prof_recv[source], prof_recv[source + 1]], 1)
        mixed = dot(both, arrived)
        mixed = mixed[0:padded] + mixed[padded : 2 * padded]
        for side in range(2):
            live = slot_ids < count_ref[0, source + side]
            mine = mixed[0:levels, side * slots : (side + 1) * slots]
            prof_ref[0, source + side] = jnp.where(live, mine, 0.0).astype(jnp.bfloat16)

    def settle(k, carry):
        peer = lax.rem(me + k, n)
        probe_copy(peer, me).wait_send()
        prof_copy(peer, me, 0, padded).wait_send()
        return carry

    lax.fori_loop(1, n, settle, 0)
    for which in range(3):
        edge_copy(which).wait_send()


def body(
    noise_seeds, diffusivity, wet_mask, vert_factor, norm_scale, obs_cell, obs_frac, obs_count
):
    rows, cols = diffusivity.shape
    levels = vert_factor.shape[0]
    n = lax.axis_size("tile")
    slots = obs_cell.shape[2]
    if rows != STEPS or n % 2 or cols & (cols - 1):
        raise ValueError("unsupported sizes")
    padded = -(-levels // 16) * 16
    span = rows + 2 * STEPS + 1
    kept = rows + 1
    f32, bf16 = jnp.float32, jnp.bfloat16
    vmem = pl.BlockSpec(memory_space=pltpu.VMEM)
    hbm = pl.BlockSpec(memory_space=pltpu.HBM)
    dma = pltpu.SemaphoreType.DMA
    return pl.pallas_call(
        functools.partial(kernel, n),
        out_shape=(
            jax.ShapeDtypeStruct((levels, rows, cols), bf16),
            jax.ShapeDtypeStruct((1, n, levels, slots), bf16),
        ),
        in_specs=[hbm] * 8,
        out_specs=(vmem, vmem),
        scratch_shapes=[
            pltpu.SMEM(noise_seeds.shape, jnp.int32),
            pltpu.SMEM(obs_count.shape, jnp.int32),
            pltpu.VMEM(diffusivity.shape, f32),
            pltpu.VMEM(wet_mask.shape, jnp.int32),
            pltpu.VMEM(vert_factor.shape, f32),
            pltpu.VMEM(norm_scale.shape, f32),
            pltpu.VMEM(obs_cell.shape, jnp.int32),
            pltpu.VMEM(obs_frac.shape, f32),
            dma((8,)),
            pltpu.VMEM((2 * rows, cols), f32),
            pltpu.VMEM((rows, cols), f32),
            pltpu.VMEM((2 * rows, cols), f32),
            pltpu.VMEM((rows, cols), f32),
            pltpu.VMEM((n, 8, slots), f32),
            pltpu.VMEM((n, 8, slots), f32),
            pltpu.VMEM((span, padded, cols), f32),
            pltpu.VMEM((span, 2 * GROUP, cols), f32),
            pltpu.VMEM((span, GROUP, cols), f32),
            pltpu.VMEM((span, GROUP, cols), f32),
            pltpu.VMEM((span, GROUP, cols // 2), f32),
            pltpu.VMEM((span, GROUP, cols), f32),
            pltpu.VMEM((kept, GROUP, cols), f32),
            pltpu.VMEM((rows, padded, cols), f32),
            pltpu.VMEM((padded, 128), f32),
            pltpu.VMEM((kept, 2 * GROUP, cols), f32),
            pltpu.VMEM((n // 2, cols, 2 * slots), bf16),
            pltpu.VMEM((n // 2, 2 * GROUP, 2 * slots), f32),
            pltpu.VMEM((rows * padded, cols), bf16),
            pltpu.VMEM((padded, rows, cols), f32),
            pltpu.VMEM((n, padded, slots), bf16),
            pltpu.VMEM((n, padded, slots), bf16),
            dma((3,)),
            dma((3,)),
            dma((n,)),
            dma((n,)),
            dma((n,)),
            dma((n,)),
        ],
        compiler_params=pltpu.CompilerParams(
            collective_id=0, has_side_effects=True, vmem_limit_bytes=60 * 1024 * 1024
        ),
    )(
        noise_seeds,
        obs_count,
        diffusivity,
        wet_mask,
        vert_factor,
        norm_scale,
        obs_cell,
        obs_frac,
    )


def solution(mesh):
    in_specs = (
        P("member"),
        P("tile", None),
        P("tile", None),
        P(),
        P("tile", None),
        P("tile", None, None),
        P("tile", None, None, None),
        P("tile", None),
    )
    out_specs = (P("member", "tile", None), P("tile", None, "member", None))
    return jax.shard_map(body, mesh=mesh, in_specs=in_specs, out_specs=out_specs, check_vma=False)
```

```python
import functools

import jax
import jax.numpy as jnp
from jax import lax
from jax.experimental import pallas as pl
from jax.experimental.pallas import tpu as pltpu
from jax.sharding import PartitionSpec as P

STEPS = 8
GROUP = 8
CHUNKS = 4
SPREAD = 3.4641016151377544
MESH = pl.DeviceIdType.MESH


def scramble(hashed):
    hashed = (hashed ^ lax.shift_right_logical(hashed, jnp.int32(16))) * jnp.int32(-2048144789)
    hashed = (hashed ^ lax.shift_right_logical(hashed, jnp.int32(13))) * jnp.int32(-1028477387)
    return hashed ^ lax.shift_right_logical(hashed, jnp.int32(16))


def kernel(
    n,
    seeds_hbm,
    count_hbm,
    diff_hbm,
    wet_hbm,
    vert_hbm,
    scale_hbm,
    cell_hbm,
    frac_hbm,
    pert_ref,
    prof_ref,
    seeds_ref,
    count_ref,
    diff_ref,
    wet_ref,
    vert_ref,
    scale_ref,
    cell_ref,
    frac_ref,
    in_sems,
    edge_send,
    above_recv,
    below_recv,
    next_recv,
    probe_send,
    probe_recv,
    noise,
    work,
    face_rows,
    face_cols,
    face_left,
    wet_all,
    scale_all,
    state,
    vert_pad,
    scaled,
    weights,
    shares,
    field,
    field_rows,
    prof_rows,
    prof_send,
    prof_recv,
    edge_ss,
    edge_rs,
    probe_ss,
    probe_rs,
    prof_ss,
    prof_rs,
):
    pulls = [
        pltpu.make_async_copy(src, dst, in_sems.at[k])
        for k, (src, dst) in enumerate(
            (
                (diff_hbm, diff_ref),
                (wet_hbm, wet_ref),
                (scale_hbm, scale_ref),
                (seeds_hbm, seeds_ref),
                (count_hbm, count_ref),
                (cell_hbm, cell_ref),
                (frac_hbm, frac_ref),
                (vert_hbm, vert_ref),
            )
        )
    ]
    for pull in pulls:
        pull.start()

    me = lax.axis_index("tile")
    rows, cols = diff_ref.shape
    half = cols // 2
    levels = vert_ref.shape[0]
    padded = state.shape[1]
    groups = padded // GROUP
    slots = cell_ref.shape[2]
    total_rows = n * rows
    span = rows + 2 * STEPS + 1
    kept = rows + 1

    barrier = pltpu.get_barrier_semaphore()

    def greet(k, carry):
        peer = lax.rem(me + k, n)
        pl.semaphore_signal(barrier, inc=1, device_id={"tile": peer}, device_id_type=MESH)
        return carry

    lax.fori_loop(1, n, greet, 0)

    for pull in pulls:
        pull.wait()

    kappa = diff_ref[...] * wet_ref[...].astype(jnp.float32)
    pair_shape = (cols, cols)
    lane = lax.broadcasted_iota(jnp.int32, pair_shape, 1)
    lane = jnp.where(lane < half, 2 * lane, 2 * lane - (cols - 1))
    split = jnp.where(lax.broadcasted_iota(jnp.int32, pair_shape, 0) == lane, 1.0, 0.0)
    plain = jnp.concatenate([kappa, scale_ref[...]], 0)
    high = plain.astype(jnp.bfloat16)
    rest = plain - high.astype(jnp.float32)
    middle = rest.astype(jnp.bfloat16)
    low = (rest - middle.astype(jnp.float32)).astype(jnp.bfloat16)
    dot = functools.partial(jnp.dot, preferred_element_type=jnp.float32)
    terms = dot(jnp.concatenate([high, middle, low], 0), split.astype(jnp.bfloat16))
    edge_send[...] = (terms[0 : 2 * rows] + terms[2 * rows : 4 * rows]) + terms[4 * rows :]
    slot_ids = lax.broadcasted_iota(jnp.int32, (1, slots), 1)

    def pack(h, carry):
        anchor = cell_ref[0, pl.ds(h, 1), :]
        frac = frac_ref[0, h]
        row = lax.shift_right_logical(anchor, jnp.int32(cols.bit_length() - 1))
        col = anchor - row * cols
        probe_send[h, 0:1, :] = col.astype(jnp.float32)
        probe_send[h, 1:2, :] = frac[1:2, :]
        probe_send[h, 2:3, :] = row.astype(jnp.float32)
        probe_send[h, 3:4, :] = frac[0:1, :]
        probe_send[h, 4:8, :] = jnp.zeros((4, slots), jnp.float32)
        return carry

    lax.fori_loop(0, n, pack, 0)

    seed_a = seeds_ref[0]
    seed_b = seeds_ref[1]
    shape = (GROUP, cols)
    col_ids = lax.broadcasted_iota(jnp.int32, shape, 1)
    col_ids = jnp.where(col_ids < half, 2 * col_ids, 2 * col_ids - (cols - 1))
    spread_ids = (
        lax.broadcasted_iota(jnp.int32, shape, 0) * (total_rows * cols) + col_ids
    ) * jnp.int32(-1640531535)
    first_row = me * rows - STEPS

    def draw(g, carry):
        at = pl.multiple_of(g * GROUP, GROUP)
        for j in range(span):
            base = (g * (GROUP * total_rows) + first_row + j) * cols
            hashed = scramble(spread_ids + (base * jnp.int32(-1640531535) + seed_a))
            hashed = scramble(hashed ^ seed_b)
            drawn = lax.shift_right_logical(hashed, jnp.int32(8)).astype(jnp.float32)
            noise[j, pl.ds(at, GROUP), :] = drawn * (SPREAD / 16777216.0) + SPREAD * (
                0.5 / 16777216.0 - 0.5
            )
        return carry

    lax.fori_loop(0, groups // 2, draw, 0)

    pl.semaphore_wait(barrier, n - 1)

    def edge_copy(which):
        if which == 0:
            src, dst, by = edge_send.at[pl.ds(0, rows)], above_recv, 1
        elif which == 1:
            src, dst, by = edge_send, below_recv, n - 1
        else:
            src, dst, by = edge_send.at[pl.ds(0, rows)], next_recv, n - 2
        return pltpu.make_async_remote_copy(
            src_ref=src,
            dst_ref=dst,
            send_sem=edge_ss.at[which],
            recv_sem=edge_rs.at[which],
            device_id={"tile": lax.rem(me + by, n)},
            device_id_type=MESH,
        )

    def probe_copy(peer, slot):
        return pltpu.make_async_remote_copy(
            src_ref=probe_send.at[peer],
            dst_ref=probe_recv.at[slot],
            send_sem=probe_ss.at[peer],
            recv_sem=probe_rs.at[slot],
            device_id={"tile": peer},
            device_id_type=MESH,
        )

    for which in range(3):
        edge_copy(which).start()

    def send_probe(k, carry):
        probe_copy(lax.rem(me + k, n), me).start()
        return carry

    lax.fori_loop(1, n, send_probe, 0)
    probe_recv[me] = probe_send[me]

    lax.fori_loop(groups // 2, groups, draw, 0)

    vert_pad[...] = jnp.zeros_like(vert_pad)
    vert_pad[0:levels, 0:levels] = vert_ref[...]
    vert = vert_pad[:, 0:padded]
    vert_hi = vert.astype(jnp.bfloat16)
    vert_lo = (vert - vert_hi.astype(jnp.float32)).astype(jnp.bfloat16)

    for which in range(3):
        edge_copy(which).wait_recv()

    zero = jnp.zeros((rows, cols), jnp.float32)
    kappa_all = jnp.concatenate(
        [
            jnp.where(me > 0, above_recv[...], zero),
            edge_send[0:rows, :],
            jnp.where(me < n - 1, below_recv[0:rows, :], zero),
            jnp.where(me < n - 2, next_recv[...], zero),
        ],
        0,
    )
    wet = jnp.where(kappa_all > 0.0, 1.0, 0.0)
    even, odd = kappa_all[:, 0:half], kappa_all[:, half:cols]
    last = lax.broadcasted_iota(jnp.int32, even.shape, 1) == half - 1
    faces_in = jnp.sqrt(even * odd)
    faces_out = jnp.where(last, 0.0, jnp.sqrt(odd * pltpu.roll(even, half - 1, 1)))
    faces_c = jnp.concatenate([faces_in, faces_out], 1)
    faces_left = pltpu.roll(faces_out, 1, 1)
    faces_r = jnp.sqrt(kappa_all[0 : span - 1] * kappa_all[1:span])
    for j in range(span):
        wet_all[j] = jnp.broadcast_to(wet[j : j + 1], shape)
        face_cols[j] = jnp.broadcast_to(faces_c[j : j + 1], shape)
        face_left[j] = jnp.broadcast_to(faces_left[j : j + 1], (GROUP, half))
        if j < span - 1:
            face_rows[j] = jnp.broadcast_to(faces_r[j : j + 1], shape)
    for r in range(kept):
        row = edge_send[rows + r : rows + r + 1] if r < rows else below_recv[rows : rows + 1]
        scale_all[r] = jnp.broadcast_to(row, shape)

    def await_probe(k, carry):
        source = lax.rem(me + k, n)
        probe_copy(source, source).wait_recv()
        return carry

    lax.fori_loop(1, n, await_probe, 0)

    pairs = n // 2
    cell_ids = lax.broadcasted_iota(jnp.int32, (cols, 2 * slots), 0)
    cell_ids = jnp.where(cell_ids < half, 2 * cell_ids, 2 * cell_ids - (cols - 1))
    cell_ids = cell_ids.astype(jnp.float32)

    def weigh(pair, carry):
        probes = jnp.concatenate([probe_recv[2 * pair], probe_recv[2 * pair + 1]], 1)
        col, frac_x, row, frac_y = probes[0:1], probes[1:2], probes[2:3], probes[3:4]
        weights[pair] = jnp.where(
            cell_ids == col, 1.0 - frac_x, jnp.where(cell_ids == col + 1.0, frac_x, 0.0)
        ).astype(jnp.bfloat16)
        for r in range(kept):
            shares[pair, r : r + 1, :] = jnp.where(
                row == float(r), 1.0 - frac_y, jnp.where(row == float(r - 1), frac_y, 0.0)
            )
        return carry

    lax.fori_loop(0, pairs, weigh, 0)

    def advance(first):
        def take(ref, j, lo):
            return ref[j, :, lo : lo + half]

        parts = [pl.ds(part * GROUP, GROUP) for part in range(2)]
        for j in range(span):
            for part in range(2):
                at = pl.multiple_of(first + part * GROUP, GROUP)
                work[j, parts[part], :] = noise[j, pl.ds(at, GROUP), :] * wet_all[j]
        for step in range(STEPS):
            here = [
                (work[step, part, 0:half], work[step, part, half:cols]) for part in parts
            ]
            up = [None, None]
            for j in range(step, span - 1 - step):
                rows_e, rows_o = take(face_rows, j, 0), take(face_rows, j, half)
                if j > step:
                    cols_in = take(face_cols, j, 0)
                    cols_right = take(face_cols, j, half)
                    cols_left = face_left[j]
                for k, part in enumerate(parts):
                    here_e, here_o = here[k]
                    next_e, next_o = work[j + 1, part, 0:half], work[j + 1, part, half:cols]
                    down_e = rows_e * (next_e - here_e)
                    down_o = rows_o * (next_o - here_o)
                    if j > step:
                        up_e, up_o = up[k]
                        inner = cols_in * (here_o - here_e)
                        right = cols_right * (pltpu.roll(here_e, half - 1, 1) - here_o)
                        left = cols_left * (here_e - pltpu.roll(here_o, 1, 1))
                        work[j, part, 0:half] = here_e + ((down_e - up_e) + (inner - left))
                        work[j, part, half:cols] = here_o + ((down_o - up_o) + (right - inner))
                    up[k] = (down_e, down_o)
                    here[k] = (next_e, next_o)

    def prof_copy(peer, slot, at, size):
        return pltpu.make_async_remote_copy(
            src_ref=prof_send.at[peer, pl.ds(at, size)],
            dst_ref=prof_recv.at[slot, pl.ds(at, size)],
            send_sem=prof_ss.at[peer],
            recv_sem=prof_rs.at[slot],
            device_id={"tile": peer},
            device_id_type=MESH,
        )

    block = 2 * GROUP
    my_pair = me // 2

    def turn(b, carry):
        first = pl.multiple_of(b * block, block)

        advance(first)
        for r in range(kept):
            for part in range(2):
                here = pl.ds(part * GROUP, GROUP)
                value = work[STEPS + r, here, :]
                if r < rows:
                    at = pl.multiple_of(first + part * GROUP, GROUP)
                    state[r, pl.ds(at, GROUP), :] = value
                scaled[r, here, :] = value * scale_all[r]
        left = scaled[...].reshape(kept * block, cols).astype(jnp.bfloat16)

        def answer(pair):
            across = jnp.dot(left, weights[pair], preferred_element_type=jnp.float32)
            total = None
            for r in range(kept):
                term = across[r * block : (r + 1) * block] * shares[pair, r : r + 1, :]
                total = term if total is None else total + term
            total = total.astype(jnp.bfloat16)
            prof_send[2 * pair, pl.ds(first, block), :] = total[:, 0:slots]
            prof_send[2 * pair + 1, pl.ds(first, block), :] = total[:, slots : 2 * slots]

        for k in range(1, pairs + 1):
            answer(lax.rem(my_pair + k, pairs))

        def send(k, inner):
            prof_copy(lax.rem(2 * my_pair + 2 + k, n), me, first, block).start()
            return inner

        lax.fori_loop(0, n - 2, send, 0)
        prof_copy(4 * my_pair + 1 - me, me, first, block).start()
        return carry

    lax.fori_loop(0, padded // block, turn, 0)
    prof_recv[me] = prof_send[me]

    for r in range(rows):
        value = state[r]
        high = value.astype(jnp.bfloat16)
        low = (value - high.astype(jnp.float32)).astype(jnp.bfloat16)
        mixed = dot(vert_hi, high) + (dot(vert_hi, low) + dot(vert_lo, high))
        scale = edge_send[rows + r : rows + r + 1, :]
        field[r * padded : (r + 1) * padded, :] = (mixed * scale).astype(jnp.bfloat16)
    lane = lax.broadcasted_iota(jnp.int32, pair_shape, 0)
    lane = jnp.where(lane < half, 2 * lane, 2 * lane - (cols - 1))
    merge = jnp.where(lax.broadcasted_iota(jnp.int32, pair_shape, 1) == lane, 1.0, 0.0)
    merge = merge.astype(jnp.bfloat16)
    for r in range(rows):
        field_rows[:, r, :] = dot(field[r * padded : (r + 1) * padded, :], merge)
    pert_ref[...] = field_rows[0:levels].astype(jnp.bfloat16)

    def await_prof(k, carry):
        source = lax.rem(me + n - k, n)
        prof_copy(source, source, 0, padded).wait_recv()
        return carry

    lax.fori_loop(1, n, await_prof, 0)

    both = jnp.concatenate([vert_hi, vert_lo], 0)
    for source in range(0, n, 2):
        arrived = jnp.concatenate([prof_recv[source], prof_recv[source + 1]], 1)
        mixed = dot(both, arrived)
        mixed = mixed[0:padded] + mixed[padded : 2 * padded]
        for side in range(2):
            live = slot_ids < count_ref[0, source + side]
            prof_rows[:, source + side, :] = jnp.where(
                live, mixed[:, side * slots : (side + 1) * slots], 0.0
            )
    prof_ref[...] = prof_rows[0:levels].astype(jnp.bfloat16)

    def settle(k, carry):
        peer = lax.rem(me + k, n)
        probe_copy(peer, me).wait_send()
        prof_copy(peer, me, 0, padded).wait_send()
        return carry

    lax.fori_loop(1, n, settle, 0)
    for which in range(3):
        edge_copy(which).wait_send()


def hand_over(pert_in, prof_in, pert_out, prof_out, sems):
    levels = pert_in.shape[0]
    size = -(-levels // CHUNKS)
    copies = []
    for k in range(CHUNKS):
        part = pl.ds(k * size, min(size, levels - k * size))
        for source, target in ((pert_in, pert_out), (prof_in, prof_out)):
            copies.append(
                pltpu.make_async_copy(source.at[part], target.at[part], sems.at[len(copies)])
            )
    for copy in copies:
        copy.start()
    for copy in copies:
        copy.wait()


def body(
    noise_seeds, diffusivity, wet_mask, vert_factor, norm_scale, obs_cell, obs_frac, obs_count
):
    rows, cols = diffusivity.shape
    levels = vert_factor.shape[0]
    n = lax.axis_size("tile")
    slots = obs_cell.shape[2]
    if rows != STEPS or n % 2 or cols & (cols - 1):
        raise ValueError("unsupported sizes")
    padded = -(-levels // 16) * 16
    span = rows + 2 * STEPS + 1
    kept = rows + 1
    f32, bf16 = jnp.float32, jnp.bfloat16
    vmem = pl.BlockSpec(memory_space=pltpu.VMEM)
    hbm = pl.BlockSpec(memory_space=pltpu.HBM)
    dma = pltpu.SemaphoreType.DMA
    perturbation, profiles = pl.pallas_call(
        functools.partial(kernel, n),
        out_shape=(
            jax.ShapeDtypeStruct((levels, rows, cols), bf16),
            jax.ShapeDtypeStruct((levels, n, slots), bf16),
        ),
        in_specs=[hbm] * 8,
        out_specs=(vmem, vmem),
        scratch_shapes=[
            pltpu.SMEM(noise_seeds.shape, jnp.int32),
            pltpu.SMEM(obs_count.shape, jnp.int32),
            pltpu.VMEM(diffusivity.shape, f32),
            pltpu.VMEM(wet_mask.shape, jnp.int32),
            pltpu.VMEM(vert_factor.shape, f32),
            pltpu.VMEM(norm_scale.shape, f32),
            pltpu.VMEM(obs_cell.shape, jnp.int32),
            pltpu.VMEM(obs_frac.shape, f32),
            dma((8,)),
            pltpu.VMEM((2 * rows, cols), f32),
            pltpu.VMEM((rows, cols), f32),
            pltpu.VMEM((2 * rows, cols), f32),
            pltpu.VMEM((rows, cols), f32),
            pltpu.VMEM((n, 8, slots), f32),
            pltpu.VMEM((n, 8, slots), f32),
            pltpu.VMEM((span, padded, cols), f32),
            pltpu.VMEM((span, 2 * GROUP, cols), f32),
            pltpu.VMEM((span, GROUP, cols), f32),
            pltpu.VMEM((span, GROUP, cols), f32),
            pltpu.VMEM((span, GROUP, cols // 2), f32),
            pltpu.VMEM((span, GROUP, cols), f32),
            pltpu.VMEM((kept, GROUP, cols), f32),
            pltpu.VMEM((rows, padded, cols), f32),
            pltpu.VMEM((padded, 128), f32),
            pltpu.VMEM((kept, 2 * GROUP, cols), f32),
            pltpu.VMEM((n // 2, cols, 2 * slots), bf16),
            pltpu.VMEM((n // 2, 2 * GROUP, 2 * slots), f32),
            pltpu.VMEM((rows * padded, cols), bf16),
            pltpu.VMEM((padded, rows, cols), f32),
            pltpu.VMEM((padded, n, slots), f32),
            pltpu.VMEM((n, padded, slots), bf16),
            pltpu.VMEM((n, padded, slots), bf16),
            dma((3,)),
            dma((3,)),
            dma((n,)),
            dma((n,)),
            dma((n,)),
            dma((n,)),
        ],
        compiler_params=pltpu.CompilerParams(
            collective_id=0, has_side_effects=True, vmem_limit_bytes=60 * 1024 * 1024
        ),
    )(
        noise_seeds,
        obs_count,
        diffusivity,
        wet_mask,
        vert_factor,
        norm_scale,
        obs_cell,
        obs_frac,
    )
    perturbation, profiles = pl.pallas_call(
        hand_over,
        out_shape=(
            jax.ShapeDtypeStruct(perturbation.shape, bf16),
            jax.ShapeDtypeStruct(profiles.shape, bf16),
        ),
        in_specs=[hbm, hbm],
        out_specs=(hbm, hbm),
        scratch_shapes=[dma((2 * CHUNKS,))],
        compiler_params=pltpu.CompilerParams(vmem_limit_bytes=60 * 1024 * 1024),
    )(perturbation, profiles)
    return (perturbation, jnp.transpose(profiles, (1, 0, 2))[None])


def solution(mesh):
    in_specs = (
        P("member"),
        P("tile", None),
        P("tile", None),
        P(),
        P("tile", None),
        P("tile", None, None),
        P("tile", None, None, None),
        P("tile", None),
    )
    out_specs = (P("member", "tile", None), P("tile", None, "member", None))
    return jax.shard_map(body, mesh=mesh, in_specs=in_specs, out_specs=out_specs, check_vma=False)
```
